256 devices in a mesh: gx: 32 (over z, x), ta: 8 (over y, core).
Axes of the slice: x: 4, y: 4, z: 8, core: 2. Of those that a mesh axis runs over, the one named last changes fastest.
Arguments:
- field: bfloat16 [1024, 8, 57344], P('ta', None, 'gx')
- weight: float32 [57344], P('gx'), may hold values from 0.2 to 2
- coef: float32 [5, 224], replicated, may hold values from -1 to 1
- window_start: int32 [32], replicated, may hold values from 0 to 247, as said below
- window_end: int32 [32], replicated, may hold values from 16 to 256, as said below
- owner_map: int32 [32], replicated, may hold values from 0 to 31, each once
Outputs:
- owned_gram: float32 [32, 1024, 1024], P('gx', 'ta')
The draws below stay inside these ranges and needn't reach their ends.
Inputs may be any that keep to these rules, and one draw needn't show every extreme that they name: `window_start`: window w starts 1 to 8 stations before w * 8, the first window at 0; some window starts exactly 8 stations before its block, and the last window starts one station before its block. `window_end`: window w ends 1 to 8 stations after (w + 1) * 8, the last window at 256; some window ends exactly 8 stations after its block. `owner_map`: each gx index owns exactly one window.
All inputs are finite; a program needn't handle non-finite values.
Results may differ from the reference program's by a relative error of at most 0.00077.
Values may be sent and summed in bfloat16 or wider, within the bound.
A program may use at most 64 MiB of HBM per device.

```python
import math
import jax
import jax.numpy as jnp
from jax import lax

STATIONS = 8
SPAN = 8
NYW = 224
BAND = 2
NT = 1024
NX = 256
WINDOWS = 32


def draw_field(key, part):
    key = jax.random.fold_in(key, 11)
    keys = jax.random.split(key, 4)
    shape = (NT, SPAN, NX * NYW)
    lead = (1, SPAN, NX * NYW)
    offset = jax.random.uniform(keys[0], lead, jnp.float32, -2.0, 2.0)
    omega = jnp.exp(jax.random.uniform(keys[1], lead, jnp.float32, math.log(0.01), 0.0))
    phase = jax.random.uniform(keys[2], lead, jnp.float32, -math.pi, math.pi)
    times = jnp.arange(NT, dtype=jnp.float32).reshape(NT, 1, 1)
    wave = 1.5 * jnp.cos(omega * times + phase)
    noise = jnp.clip(jax.random.normal(keys[3], shape, jnp.float32), -4.0, 4.0)
    return (offset + wave + noise).astype(jnp.bfloat16)


def draw_window_start(key, part):
    key = jax.random.fold_in(key, 21)
    reach = jax.random.randint(key, (WINDOWS,), 1, STATIONS + 1)
    index = jnp.arange(WINDOWS, dtype=jnp.int32)
    reach = jnp.where(index == WINDOWS - 1, 1, reach)
    reach = jnp.where(index == 1, STATIONS, reach)
    reach = jnp.where(index == 0, 0, reach)
    return (index * STATIONS - reach).astype(jnp.int32)


def draw_window_end(key, part):
    key = jax.random.fold_in(key, 22)
    reach = jax.random.randint(key, (WINDOWS,), 1, STATIONS + 1)
    index = jnp.arange(WINDOWS, dtype=jnp.int32)
    reach = jnp.where(index == 0, STATIONS, reach)
    reach = jnp.where(index == WINDOWS - 1, 0, reach)
    return ((index + 1) * STATIONS + reach).astype(jnp.int32)


def levels(rng, shape, cuts, low, top_value):
    level = 1.0
    for position, parts in cuts:
        steps = jax.random.uniform(jax.random.fold_in(jax.random.fold_in(rng, 6), position), (parts,), jnp.float32, low / len(cuts), top_value / len(cuts))
        level = level * jnp.repeat(jnp.exp(steps), shape[position] // parts).reshape((-1,) + (1,) * (len(shape) - 1 - position))
    return level


def setup_inputs(seed: int = 0) -> dict:
    streams_of = jax.random.split(jax.random.key(seed), 7)
    return {
        "field": draw_field(jax.random.fold_in(streams_of[6], 71), 0),
        "weight": jnp.clip(jnp.exp(math.log(2.0) - 2.3025851 * jax.random.uniform(streams_of[1], (NX * NYW,), jnp.float32) ** levels(streams_of[1], (NX * NYW,), ((0, 32),), -0.2, 0.2)), 0.2, 2.0),
        "coef": jnp.clip(jax.random.uniform(streams_of[2], (2 * BAND + 1, NYW), jnp.float32, -1.0, 1.0), -1.0, 1.0),
        "window_start": draw_window_start(jax.random.fold_in(streams_of[6], 71), 0),
        "window_end": draw_window_end(jax.random.fold_in(streams_of[6], 71), 0),
        "owner_map": jax.random.permutation(streams_of[5], WINDOWS).astype(jnp.int32),
    }


def prepare(block, weight_block, coef):
    values = block.astype(jnp.float32)
    centered = values - lax.optimization_barrier(jnp.mean(values, axis=0, keepdims=True))
    shaped = centered.reshape(NT, SPAN, STATIONS, NYW)
    padded = jnp.pad(shaped, ((0, 0), (0, 0), (0, 0), (BAND, BAND)))
    filtered = jnp.zeros(shaped.shape, jnp.float32)
    for offset in range(2 * BAND + 1):
        filtered = filtered + coef[offset] * padded[..., offset:offset + NYW]
    factor = jnp.sqrt(weight_block).reshape(STATIONS, NYW)
    return (filtered * factor).astype(jnp.bfloat16).reshape(NT, SPAN, STATIONS * NYW)

def reference(field, weight, coef, window_start, window_end, owner_map):
    width = STATIONS * NYW

    def one_block(index):
        block = lax.dynamic_slice_in_dim(field, index * width, width, 2)
        weight_block = lax.dynamic_slice_in_dim(weight, index * width, width, 0)
        return prepare(block, weight_block, coef)
    scaled = lax.map(one_block, jnp.arange(WINDOWS, dtype=jnp.int32))
    zero = jnp.zeros_like(scaled[:1])
    padded = jnp.concatenate([zero, scaled, zero], axis=0)

    def window_gram(index):
        wide = lax.dynamic_slice_in_dim(padded, index, 3, 0)
        stations = (index - 1) * STATIONS + jnp.arange(3 * STATIONS, dtype=jnp.int32)
        inside = (stations >= window_start[index]) & (stations < window_end[index])
        mask = jnp.repeat(inside, NYW).reshape(3, width).astype(jnp.bfloat16)
        masked = wide * mask[:, None, None, :]
        left = masked.transpose(1, 0, 2, 3).reshape(NT, 3 * SPAN * width)
        right = wide.transpose(1, 0, 2, 3).reshape(NT, 3 * SPAN * width)
        total = jnp.dot(left, right.T, preferred_element_type=jnp.float32)
        count = ((window_end[index] - window_start[index]) * SPAN * NYW).astype(jnp.float32)
        return total / count
    grams = lax.map(window_gram, jnp.arange(WINDOWS, dtype=jnp.int32))
    return jnp.zeros_like(grams).at[owner_map].set(grams)
```

```python
import jax
import jax.numpy as jnp
from jax import lax
from jax.sharding import PartitionSpec as P

SPAN = 8
NYW = 224
BAND = 2


def padded_2(block, sides, width):
    for axis, dim in sides:
        count = lax.axis_size(axis)
        forward = [(i, i + 1) for i in range(count - 1)]
        backward = [(target, source) for source, target in forward]
        low = lax.ppermute(
            lax.slice_in_dim(block, block.shape[dim] - width, None, axis=dim), axis, forward
        )
        high = lax.ppermute(lax.slice_in_dim(block, 0, width, axis=dim), axis, backward)
        block = jnp.concatenate([low, block, high], axis=dim)
    return block


def station_mask(begin, count, lower, upper):
    stations = begin + jnp.arange(count, dtype=jnp.int32)
    inside = (stations >= lower) & (stations < upper)
    return jnp.repeat(inside, NYW).astype(jnp.bfloat16)


def on_device(field, weight, coef, window_start, window_end, owner_map):
    lines = lax.all_to_all(field, "ta", split_axis=1, concat_axis=0, tiled=True)
    total = lines.shape[0]
    span_local = lines.shape[1]
    width = lines.shape[2]
    stations = width // NYW
    values = lines.astype(jnp.float32)
    centered = values - jnp.mean(values, axis=0, keepdims=True)
    shaped = centered.reshape(total, span_local, stations, NYW)
    padded = jnp.pad(shaped, ((0, 0), (0, 0), (0, 0), (BAND, BAND)))
    filtered = jnp.zeros(shaped.shape, jnp.float32)
    for offset in range(2 * BAND + 1):
        filtered = filtered + coef[offset] * padded[..., offset : offset + NYW]
    factor = jnp.sqrt(weight).reshape(stations, NYW)
    scaled = (filtered * factor).astype(jnp.bfloat16).reshape(total, span_local, width)
    place = lax.axis_index("gx")
    first = window_start[place]
    last = window_end[place]
    wide = padded_2(scaled, (("gx", 2),), width)
    mask = station_mask((place - 1) * stations, 3 * stations, first, last)
    partial_value = jnp.einsum("tsf,usf->tu", wide * mask, wide, preferred_element_type=jnp.float32)
    rows = lax.psum_scatter(partial_value, "ta", scatter_dimension=0, tiled=True)
    gram = rows / ((last - first) * SPAN * NYW).astype(jnp.float32)
    groups = lax.axis_size("gx")
    order = jnp.arange(groups, dtype=jnp.int32)
    source = jnp.sum(jnp.where(owner_map[None, :] == order[:, None], order[None, :], 0), axis=1)
    pieces = gram.reshape(groups, gram.shape[0] // groups, gram.shape[1])
    spread = lax.all_to_all(pieces, "gx", split_axis=0, concat_axis=0, tiled=True)
    sorted_pieces = jnp.concatenate(
        [lax.dynamic_slice_in_dim(spread, source[d], 1, axis=0) for d in range(groups)], axis=0
    )
    owned = lax.all_to_all(sorted_pieces, "gx", split_axis=0, concat_axis=0, tiled=True)
    owned = owned.reshape(gram.shape)
    return owned[None]


def solution(mesh):
    placed = (P("ta", None, "gx"), P("gx"), P(), P(), P(), P())
    return jax.shard_map(
        on_device, mesh=mesh, in_specs=placed, out_specs=P("gx", "ta", None), check_vma=False
    )
```

```python
import functools

import jax
import jax.numpy as jnp
from jax import lax
from jax.experimental import pallas as pl
from jax.experimental.pallas import tpu as pltpu
from jax.sharding import PartitionSpec as P

SPAN = 8
NYW = 224
BAND = 2
STATIONS = 8
WIDTH = STATIONS * NYW
TA = 8
MESH = pl.DeviceIdType.MESH
CUTS = (0, 384, 896, 1280, 1792)
CHUNKS = len(CUTS) - 1
KEPT = 5
PAIR = 6


def rotated(me, step, count):
    return lax.rem(me + step, count)


def gram_kernel(
    rows, total, x_ref, taps_ref, part_ref, out_ref,
    sums, send, lines, gram, landed,
    sum_send, sum_recv, line_send, line_recv, line_own, gram_send, gram_recv, gram_own,
):
    place = lax.axis_index("gx")
    me = lax.axis_index("ta")
    wide = KEPT * rows

    for span in range(SPAN):
        def add(step, acc):
            start = pl.multiple_of(step * 16, 16)
            tile = x_ref[span, pl.ds(start, 16), :].astype(jnp.float32)
            return acc + tile[:8] + tile[8:]
        acc = lax.fori_loop(0, rows // 16, add, jnp.zeros((8, WIDTH), jnp.float32))
        sums[me, pl.ds(span, 1), :] = jnp.sum(acc, axis=0, keepdims=True)

    barrier = pltpu.get_barrier_semaphore()

    @pl.loop(1, TA)
    def _(step):
        pl.semaphore_signal(
            barrier, inc=1, device_id=(place, rotated(me, step, TA)), device_id_type=MESH
        )
    pl.semaphore_wait(barrier, TA - 1)

    def sum_copy(owner, target):
        return pltpu.make_async_remote_copy(
            src_ref=sums.at[owner], dst_ref=sums.at[owner],
            send_sem=sum_send.at[target], recv_sem=sum_recv.at[owner],
            device_id=(place, target), device_id_type=MESH,
        )

    @pl.loop(1, TA)
    def _(step):
        sum_copy(me, rotated(me, step, TA)).start()

    @pl.loop(1, TA)
    def _(step):
        sum_copy(rotated(me, step, TA), me).wait_recv()

    mean = jnp.sum(sums[...], axis=0) * (1.0 / total)

    def line_copy(chunk, owner, target):
        lanes = slice(CUTS[chunk], CUTS[chunk + 1])
        return pltpu.make_async_remote_copy(
            src_ref=send.at[target, :, lanes],
            dst_ref=lines.at[pl.ds(pl.multiple_of(owner * rows, rows), rows), lanes],
            send_sem=line_send.at[chunk, target], recv_sem=line_recv.at[chunk, owner],
            device_id=(place, target), device_id_type=MESH,
        )

    def own_copy(chunk):
        lanes = slice(CUTS[chunk], CUTS[chunk + 1])
        return pltpu.make_async_copy(
            send.at[me, :, lanes],
            lines.at[pl.ds(pl.multiple_of(me * rows, rows), rows), lanes],
            line_own.at[chunk],
        )

    for chunk in range(CHUNKS):
        for span in (2 * chunk, 2 * chunk + 1):
            level = mean[span : span + 1]

            @pl.loop(0, rows // 16)
            def _(step):
                start = pl.multiple_of(step * 16, 16)
                centered = x_ref[span, pl.ds(start, 16), :].astype(jnp.float32) - level
                filtered = taps_ref[BAND : BAND + 1, :] * centered
                for offset in range(2 * BAND + 1):
                    if offset != BAND:
                        moved = pltpu.roll(centered, (BAND - offset) % WIDTH, 1)
                        filtered = filtered + taps_ref[offset : offset + 1, :] * moved
                scaled = filtered.astype(jnp.bfloat16)
                for station in range(STATIONS):
                    send[station, pl.ds(start, 16), NYW * span : NYW * (span + 1)] = scaled[
                        :, NYW * station : NYW * (station + 1)
                    ]

        @pl.loop(1, TA)
        def _(step):
            line_copy(chunk, me, rotated(me, step, TA)).start()
        own_copy(chunk).start()

    def gram_copy(owner, target):
        source = gram.at[
            pl.ds(pl.multiple_of(target * rows, rows), rows),
            pl.ds(pl.multiple_of(lax.rem(target, 2) * rows, rows), wide),
        ]
        return pltpu.make_async_remote_copy(
            src_ref=source, dst_ref=landed.at[owner],
            send_sem=gram_send.at[target], recv_sem=gram_recv.at[owner],
            device_id=(place, target), device_id_type=MESH,
        )

    def gram_local():
        source = gram.at[
            pl.ds(pl.multiple_of(me * rows, rows), rows),
            pl.ds(pl.multiple_of(lax.rem(me, 2) * rows, rows), wide),
        ]
        return pltpu.make_async_copy(source, landed.at[me], gram_own)

    pair = 2 * rows
    for chunk in range(CHUNKS):
        lanes = slice(CUTS[chunk], CUTS[chunk + 1])
        own_copy(chunk).wait()

        @pl.loop(1, TA)
        def _(step):
            line_copy(chunk, rotated(me, step, TA), me).wait_recv()

        @pl.loop(1, TA // 2 + 1)
        def _(step):
            row = lax.rem(me // 2 + step, TA // 2)
            where = pl.ds(pl.multiple_of(row * pair, pair), pair)
            left = lines[where, lanes]
            for block in range(PAIR // 2):
                column = lax.rem(row + block, TA // 2)
                right = lines[pl.ds(pl.multiple_of(column * pair, pair), pair), lanes]
                product = lax.dot_general(
                    left, right, (((1,), (1,)), ((), ())), preferred_element_type=jnp.float32
                )
                at = slice(block * pair, (block + 1) * pair)
                if chunk == 0:
                    gram[where, at] = product
                else:
                    gram[where, at] = gram[where, at] + product
            if chunk == CHUNKS - 1:
                for side in range(2):
                    target = 2 * row + side

                    @pl.when(target != me)
                    def _():
                        gram_copy(me, target).start()

    gram_local().start()
    gram_local().wait()

    @pl.loop(0, rows // 8)
    def _(step):
        at = pl.ds(pl.multiple_of(step * 8, 8), 8)
        tile = landed[me, at, :]
        out_ref[0, at, :] = tile
        out_ref[1, at, :] = tile * part_ref[0, me]
        out_ref[2, at, :] = tile * part_ref[1, me]

    @pl.loop(1, TA)
    def _(count):
        owner = rotated(me, TA - count, TA)
        gram_copy(owner, me).wait_recv()
        upper = part_ref[0, owner]
        lower = part_ref[1, owner]

        @pl.loop(0, rows // 8)
        def _(step):
            at = pl.ds(pl.multiple_of(step * 8, 8), 8)
            tile = landed[owner, at, :]
            out_ref[0, at, :] = out_ref[0, at, :] + tile
            out_ref[1, at, :] = out_ref[1, at, :] + tile * upper
            out_ref[2, at, :] = out_ref[2, at, :] + tile * lower

    @pl.loop(1, TA)
    def _(step):
        target = rotated(me, step, TA)
        sum_copy(me, target).wait_send()
        gram_copy(me, target).wait_send()
        for chunk in range(CHUNKS):
            line_copy(chunk, me, target).wait_send()


def owner_kernel(
    groups, rows, sums_ref, source_ref, count_ref, out_ref,
    beside, pieces, spread, ordered, owned, block, turned,
    side_send, side_recv, out_send, out_recv, back_send, back_recv, turn_send, turn_recv, own_sem,
):
    place = lax.axis_index("gx")
    me = lax.axis_index("ta")
    piece = rows // groups
    turns = TA - KEPT

    barrier = pltpu.get_barrier_semaphore()

    @pl.loop(1, groups)
    def _(step):
        pl.semaphore_signal(
            barrier, inc=1, device_id=(rotated(place, step, groups), me), device_id_type=MESH
        )
    for turn in range(1, turns + 1):
        for other in (rotated(me, turn, TA), rotated(me, TA - turn, TA)):
            pl.semaphore_signal(barrier, inc=1, device_id=(place, other), device_id_type=MESH)
    pl.semaphore_wait(barrier, groups - 1 + 2 * turns)

    after = rotated(place, 1, groups)
    before = rotated(place, groups - 1, groups)

    def side_copy(side):
        return pltpu.make_async_remote_copy(
            src_ref=sums_ref.at[1 + side], dst_ref=beside.at[side],
            send_sem=side_send.at[side], recv_sem=side_recv.at[side],
            device_id=((after, before)[side], me), device_id_type=MESH,
        )

    for side in range(2):
        side_copy(side).start()
    for side in range(2):
        side_copy(side).wait()

    @pl.loop(0, rows // 8)
    def _(step):
        at = pl.ds(pl.multiple_of(step * 8, 8), 8)
        tile = (sums_ref[0, at, :] + beside[0, at, :] + beside[1, at, :]) / count_ref[0]
        for part in range(8 // piece):
            pieces[step * (8 // piece) + part] = tile[part * piece : (part + 1) * piece]

    def out_copy(owner, target):
        return pltpu.make_async_remote_copy(
            src_ref=pieces.at[target], dst_ref=spread.at[owner],
            send_sem=out_send.at[target], recv_sem=out_recv.at[owner],
            device_id=(target, me), device_id_type=MESH,
        )

    @pl.loop(1, groups)
    def _(step):
        out_copy(place, rotated(place, step, groups)).start()
    own = pltpu.make_async_copy(pieces.at[place], spread.at[place], own_sem.at[0])
    own.start()
    own.wait()

    @pl.loop(1, groups)
    def _(step):
        out_copy(rotated(place, groups - step, groups), place).wait_recv()

    @pl.loop(0, groups)
    def _(slot):
        ordered[slot] = spread[source_ref[slot]]

    def back_copy(owner, target):
        return pltpu.make_async_remote_copy(
            src_ref=ordered.at[target], dst_ref=owned.at[owner],
            send_sem=back_send.at[target], recv_sem=back_recv.at[owner],
            device_id=(target, me), device_id_type=MESH,
        )

    @pl.loop(1, groups)
    def _(step):
        back_copy(place, rotated(place, step, groups)).start()
    back = pltpu.make_async_copy(ordered.at[place], owned.at[place], own_sem.at[1])
    back.start()
    back.wait()

    @pl.loop(1, groups)
    def _(step):
        back_copy(rotated(place, groups - step, groups), place).wait_recv()

    @pl.loop(0, rows // 8)
    def _(step):
        at = pl.ds(pl.multiple_of(step * 8, 8), 8)
        for part in range(8 // piece):
            tile = owned[step * (8 // piece) + part]
            for column in range(KEPT):
                block[column, pl.ds(step * 8 + part * piece, piece), :] = tile[
                    :, column * rows : (column + 1) * rows
                ]

    def turn_copy(turn):
        return pltpu.make_async_remote_copy(
            src_ref=block.at[turn], dst_ref=turned.at[turn - 1],
            send_sem=turn_send.at[turn - 1], recv_sem=turn_recv.at[turn - 1],
            device_id=(place, rotated(me, turn, TA)), device_id_type=MESH,
        )

    for turn in range(1, turns + 1):
        turn_copy(turn).start()
    for column in range(KEPT):
        target = rotated(me, column, TA)
        out_ref[:, pl.ds(pl.multiple_of(target * rows, rows), rows)] = block[column]
    for turn in range(1, turns + 1):
        turn_copy(turn).wait()
        target = rotated(me, TA - turn, TA)
        out_ref[:, pl.ds(pl.multiple_of(target * rows, rows), rows)] = turned[turn - 1].T

    @pl.loop(1, groups)
    def _(step):
        target = rotated(place, step, groups)
        out_copy(place, target).wait_send()
        back_copy(place, target).wait_send()


def on_device(field, weight, coef, window_start, window_end, owner_map):
    rows = field.shape[0]
    groups = lax.axis_size("gx")
    piece = rows // groups
    total = rows * TA
    place = lax.axis_index("gx")

    lines = jnp.transpose(field, (1, 0, 2))
    point = jnp.arange(NYW, dtype=jnp.int32)[None, :]
    reach = point + jnp.arange(-BAND, BAND + 1, dtype=jnp.int32)[:, None]
    taps = jnp.where((reach >= 0) & (reach < NYW), coef, 0.0)
    taps = jnp.tile(taps, (1, STATIONS)) * jnp.sqrt(weight)[None, :]

    station = place * STATIONS + jnp.arange(STATIONS, dtype=jnp.int32)
    next_start = jnp.where(
        place + 1 < groups, window_start[jnp.minimum(place + 1, groups - 1)], groups * STATIONS
    )
    last_end = jnp.where(place > 0, window_end[jnp.maximum(place - 1, 0)], 0)
    part = jnp.stack([station >= next_start, station < last_end]).astype(jnp.float32)
    count = ((window_end[place] - window_start[place]) * SPAN * NYW).astype(jnp.float32)
    order = jnp.arange(groups, dtype=jnp.int32)
    source = jnp.sum(jnp.where(owner_map[None, :] == order[:, None], order[None, :], 0), axis=1)

    vmem = pl.BlockSpec(memory_space=pltpu.VMEM)
    smem = pl.BlockSpec(memory_space=pltpu.SMEM)
    dma = pltpu.SemaphoreType.DMA
    wide = KEPT * rows
    sums = pl.pallas_call(
        functools.partial(gram_kernel, rows, total),
        out_shape=jax.ShapeDtypeStruct((3, rows, wide), jnp.float32),
        in_specs=[vmem, vmem, smem],
        out_specs=vmem,
        scratch_shapes=[
            pltpu.VMEM((TA, SPAN, WIDTH), jnp.float32),
            pltpu.VMEM((TA, rows, WIDTH), jnp.bfloat16),
            pltpu.VMEM((total, WIDTH), jnp.bfloat16),
            pltpu.VMEM((total, PAIR * rows), jnp.float32),
            pltpu.VMEM((TA, rows, wide), jnp.float32),
            dma((TA,)), dma((TA,)),
            dma((CHUNKS, TA)), dma((CHUNKS, TA)), dma((CHUNKS,)),
            dma((TA,)), dma((TA,)), dma,
        ],
        compiler_params=pltpu.CompilerParams(
            collective_id=0, has_side_effects=True, vmem_limit_bytes=48 * 1024 * 1024
        ),
        name="station_gram",
    )(lines, taps, part)

    turns = TA - KEPT
    owned = pl.pallas_call(
        functools.partial(owner_kernel, groups, rows),
        out_shape=jax.ShapeDtypeStruct((rows, total), jnp.float32),
        in_specs=[vmem, smem, smem],
        out_specs=vmem,
        scratch_shapes=[
            pltpu.VMEM((2, rows, wide), jnp.float32),
            pltpu.VMEM((groups, piece, wide), jnp.float32),
            pltpu.VMEM((groups, piece, wide), jnp.float32),
            pltpu.VMEM((groups, piece, wide), jnp.float32),
            pltpu.VMEM((groups, piece, wide), jnp.float32),
            pltpu.VMEM((KEPT, rows, rows), jnp.float32),
            pltpu.VMEM((turns, rows, rows), jnp.float32),
            dma((2,)), dma((2,)), dma((groups,)), dma((groups,)),
            dma((groups,)), dma((groups,)), dma((turns,)), dma((turns,)), dma((2,)),
        ],
        compiler_params=pltpu.CompilerParams(
            collective_id=1, has_side_effects=True, vmem_limit_bytes=32 * 1024 * 1024
        ),
        name="owner_rows",
    )(sums, source, count[None])
    return owned[None]


def solution(mesh):
    placed = (P("ta", None, "gx"), P("gx"), P(), P(), P(), P())
    return jax.shard_map(
        on_device, mesh=mesh, in_specs=placed, out_specs=P("gx", "ta", None), check_vma=False
    )
```

```python
import functools

import jax
import jax.numpy as jnp
from jax import lax
from jax.experimental import pallas as pl
from jax.experimental.pallas import tpu as pltpu
from jax.sharding import PartitionSpec as P

SPAN = 8
NYW = 224
BAND = 2
STATIONS = 8
WIDTH = STATIONS * NYW
TA = 8
MESH = pl.DeviceIdType.MESH
SENT = ((0, 1), (2, 3), (4, 5), (6,), (7,))
CUTS = (0, 384, 896, 1280, 1536, 1792)
DONE = (0, 256, 896, 1152, 1408, 1792)
CHUNKS = len(SENT)
AHEAD = 2
KEPT = 5
PAIR = 6


def rotated(me, step, count):
    return lax.rem(me + step, count)


def gram_kernel(
    rows, total, groups, x_ref, weight_ref, coef_ref, start_ref, end_ref, out_ref,
    send, lines, scaled, taps, mean, base, gram, landed,
    line_send, line_recv, line_own, gram_send, gram_recv, gram_own,
):
    place = lax.axis_index("gx")
    me = lax.axis_index("ta")
    wide = KEPT * rows
    tall = 2 * rows

    barrier = pltpu.get_barrier_semaphore()

    @pl.loop(1, TA)
    def _(step):
        pl.semaphore_signal(
            barrier, inc=1, device_id=(place, rotated(me, step, TA)), device_id_type=MESH
        )

    def line_copy(chunk, owner, target):
        lanes = slice(CUTS[chunk], CUTS[chunk + 1])
        return pltpu.make_async_remote_copy(
            src_ref=send.at[target, :, lanes],
            dst_ref=lines.at[pl.ds(pl.multiple_of(owner * rows, rows), rows), lanes],
            send_sem=line_send.at[chunk, target], recv_sem=line_recv.at[chunk, owner],
            device_id=(place, target), device_id_type=MESH,
        )

    def own_copy(chunk):
        lanes = slice(CUTS[chunk], CUTS[chunk + 1])
        return pltpu.make_async_copy(
            send.at[me, :, lanes],
            lines.at[pl.ds(pl.multiple_of(me * rows, rows), rows), lanes],
            line_own.at[chunk],
        )

    def start_lines(chunk):
        @pl.loop(1, TA)
        def _(step):
            line_copy(chunk, me, rotated(me, step, TA)).start()

    for chunk in range(CHUNKS):
        for span in SENT[chunk]:

            @pl.loop(0, rows // 16)
            def _(step):
                start = pl.multiple_of(step * 16, 16)
                tile = x_ref[span, pl.ds(start, 16), :]
                for station in range(STATIONS):
                    send[station, pl.ds(start, 16), NYW * span : NYW * (span + 1)] = tile[
                        :, NYW * station : NYW * (station + 1)
                    ]

        if chunk == 0:
            pl.semaphore_wait(barrier, TA - 1)

        if chunk < AHEAD:
            start_lines(chunk)
        own_copy(chunk).start()

    weight = jnp.zeros((1, NYW), jnp.float32)
    for station in range(STATIONS):
        weight = jnp.where(
            me == station, weight_ref[:, NYW * station : NYW * (station + 1)], weight
        )
    reach = (
        lax.broadcasted_iota(jnp.int32, (2 * BAND + 1, NYW), 1)
        + lax.broadcasted_iota(jnp.int32, (2 * BAND + 1, NYW), 0) - BAND
    )
    tap = jnp.where((reach >= 0) & (reach < NYW), coef_ref[...], 0.0) * jnp.sqrt(weight)
    for span in range(SPAN):
        taps[:, NYW * span : NYW * (span + 1)] = tap

    def gram_copy(owner, target):
        source = gram.at[
            pl.ds(pl.multiple_of(target * rows, rows), rows),
            pl.ds(pl.multiple_of(lax.rem(target, 2) * rows, rows), wide),
        ]
        return pltpu.make_async_remote_copy(
            src_ref=source, dst_ref=landed.at[owner],
            send_sem=gram_send.at[target], recv_sem=gram_recv.at[owner],
            device_id=(place, target), device_id_type=MESH,
        )

    def gram_local():
        source = gram.at[
            pl.ds(pl.multiple_of(me * rows, rows), rows),
            pl.ds(pl.multiple_of(lax.rem(me, 2) * rows, rows), wide),
        ]
        return pltpu.make_async_copy(source, landed.at[me], gram_own)

    pair = 2 * rows
    for chunk in range(CHUNKS):
        own_copy(chunk).wait()

        @pl.loop(1, TA)
        def _(step):
            line_copy(chunk, rotated(me, step, TA), me).wait_recv()

        if chunk + AHEAD < CHUNKS:

            @pl.loop(1, TA)
            def _(step):
                line_copy(chunk, me, rotated(me, step, TA)).wait_send()
            start_lines(chunk + AHEAD)

        new = slice(CUTS[chunk], CUTS[chunk + 1])
        fresh = CUTS[chunk + 1] - CUTS[chunk]

        def add(step, acc):
            start = pl.multiple_of(step * 16, 16)
            tile = lines[pl.ds(start, 16), new].astype(jnp.float32)
            return acc + tile
        acc = lax.fori_loop(0, total // 16, add, jnp.zeros((16, fresh), jnp.float32))
        mean[:, new] = jnp.sum(acc, axis=0, keepdims=True) * (1.0 / total)

        first, last = DONE[chunk], DONE[chunk + 1]
        low = first if first % (4 * NYW) == 0 else first - 128
        high = last if last % (4 * NYW) == 0 else last + 128
        lanes = slice(first, last)

        middle = slice(first - low, last - low)
        level = mean[:, low:high]
        offset_level = jnp.zeros((1, last - first), jnp.float32)
        for offset in range(2 * BAND + 1):
            moved = level if offset == BAND else pltpu.roll(level, (BAND - offset) % (high - low), 1)
            offset_level = offset_level + taps[offset : offset + 1, lanes] * moved[:, middle]
        base[:, lanes] = offset_level

        @pl.loop(0, total // tall)
        def _(step):
            at = pl.ds(pl.multiple_of(step * tall, tall), tall)
            raw = lines[at, low:high]
            filtered = taps[BAND : BAND + 1, lanes] * raw[:, middle].astype(jnp.float32)
            for offset in range(2 * BAND + 1):
                if offset != BAND:
                    moved = pltpu.roll(raw, (BAND - offset) % (high - low), 1)[:, middle]
                    filtered = filtered + taps[offset : offset + 1, lanes] * moved.astype(jnp.float32)
            scaled[at, lanes] = (filtered - base[:, lanes]).astype(jnp.bfloat16)

        @pl.loop(1, TA // 2 + 1)
        def _(step):
            row = lax.rem(me // 2 + step, TA // 2)
            where = pl.ds(pl.multiple_of(row * pair, pair), pair)
            left = scaled[where, lanes]
            for block in range(PAIR // 2):
                column = lax.rem(row + block, TA // 2)
                right = scaled[pl.ds(pl.multiple_of(column * pair, pair), pair), lanes]
                product = lax.dot_general(
                    left, right, (((1,), (1,)), ((), ())), preferred_element_type=jnp.float32
                )
                at = slice(block * pair, (block + 1) * pair)
                if chunk == 0:
                    gram[where, at] = product
                else:
                    gram[where, at] = gram[where, at] + product
            if chunk == CHUNKS - 1:
                for side in range(2):
                    target = 2 * row + side

                    @pl.when(target != me)
                    def _():
                        gram_copy(me, target).start()

    gram_local().start()
    gram_local().wait()

    next_start = jnp.where(
        place + 1 < groups, start_ref[jnp.minimum(place + 1, groups - 1)], groups * STATIONS
    )
    last_end = jnp.where(place > 0, end_ref[jnp.maximum(place - 1, 0)], 0)

    def shares(owner):
        station = place * STATIONS + owner
        upper = jnp.where(station >= next_start, 1.0, 0.0)
        lower = jnp.where(station < last_end, 1.0, 0.0)
        return upper, lower

    upper, lower = shares(me)

    @pl.loop(0, rows // 8)
    def _(step):
        at = pl.ds(pl.multiple_of(step * 8, 8), 8)
        tile = landed[me, at, :]
        out_ref[0, at, :] = tile
        out_ref[1, at, :] = tile * upper
        out_ref[2, at, :] = tile * lower

    @pl.loop(1, TA)
    def _(count):
        owner = rotated(me, TA - count, TA)
        gram_copy(owner, me).wait_recv()
        upper, lower = shares(owner)

        @pl.loop(0, rows // 8)
        def _(step):
            at = pl.ds(pl.multiple_of(step * 8, 8), 8)
            tile = landed[owner, at, :]
            out_ref[0, at, :] = out_ref[0, at, :] + tile
            out_ref[1, at, :] = out_ref[1, at, :] + tile * upper
            out_ref[2, at, :] = out_ref[2, at, :] + tile * lower

    @pl.loop(1, TA)
    def _(step):
        target = rotated(me, step, TA)
        gram_copy(me, target).wait_send()
        for chunk in range(CHUNKS - AHEAD, CHUNKS):
            line_copy(chunk, me, target).wait_send()


def owner_kernel(
    groups, rows, sums_ref, start_ref, end_ref, owner_ref, out_ref,
    source,
    beside, pieces, spread, ordered, owned, block, turned,
    side_send, side_recv, out_send, out_recv, back_send, back_recv, turn_send, turn_recv, own_sem,
):
    place = lax.axis_index("gx")
    me = lax.axis_index("ta")
    piece = rows // groups
    turns = TA - KEPT

    barrier = pltpu.get_barrier_semaphore()

    @pl.loop(1, groups)
    def _(step):
        pl.semaphore_signal(
            barrier, inc=1, device_id=(rotated(place, step, groups), me), device_id_type=MESH
        )
    for turn in range(1, turns + 1):
        for other in (rotated(me, turn, TA), rotated(me, TA - turn, TA)):
            pl.semaphore_signal(barrier, inc=1, device_id=(place, other), device_id_type=MESH)
    pl.semaphore_wait(barrier, groups - 1 + 2 * turns)

    after = rotated(place, 1, groups)
    before = rotated(place, groups - 1, groups)

    def side_copy(side):
        return pltpu.make_async_remote_copy(
            src_ref=sums_ref.at[1 + side], dst_ref=beside.at[side],
            send_sem=side_send.at[side], recv_sem=side_recv.at[side],
            device_id=((after, before)[side], me), device_id_type=MESH,
        )

    for side in range(2):
        side_copy(side).start()

    @pl.loop(0, groups)
    def _(slot):
        window = jnp.int32(0)
        for step in range(groups):
            window = jnp.where(owner_ref[step] == slot, step, window)
        source[slot] = window
    count = ((end_ref[place] - start_ref[place]) * (SPAN * NYW)).astype(jnp.float32)

    for side in range(2):
        side_copy(side).wait()

    @pl.loop(0, rows // 8)
    def _(step):
        at = pl.ds(pl.multiple_of(step * 8, 8), 8)
        tile = (sums_ref[0, at, :] + beside[0, at, :] + beside[1, at, :]) / count
        for part in range(8 // piece):
            pieces[step * (8 // piece) + part] = tile[part * piece : (part + 1) * piece]

    def out_copy(owner, target):
        return pltpu.make_async_remote_copy(
            src_ref=pieces.at[target], dst_ref=spread.at[owner],
            send_sem=out_send.at[target], recv_sem=out_recv.at[owner],
            device_id=(target, me), device_id_type=MESH,
        )

    @pl.loop(1, groups)
    def _(step):
        out_copy(place, rotated(place, step, groups)).start()
    own = pltpu.make_async_copy(pieces.at[place], spread.at[place], own_sem.at[0])
    own.start()
    own.wait()

    @pl.loop(1, groups)
    def _(step):
        out_copy(rotated(place, groups - step, groups), place).wait_recv()

    @pl.loop(0, groups)
    def _(slot):
        ordered[slot] = spread[source[slot]]

    def back_copy(owner, target):
        return pltpu.make_async_remote_copy(
            src_ref=ordered.at[target], dst_ref=owned.at[owner],
            send_sem=back_send.at[target], recv_sem=back_recv.at[owner],
            device_id=(target, me), device_id_type=MESH,
        )

    @pl.loop(1, groups)
    def _(step):
        back_copy(place, rotated(place, step, groups)).start()
    back = pltpu.make_async_copy(ordered.at[place], owned.at[place], own_sem.at[1])
    back.start()
    back.wait()

    @pl.loop(1, groups)
    def _(step):
        back_copy(rotated(place, groups - step, groups), place).wait_recv()

    @pl.loop(0, rows // 8)
    def _(step):
        at = pl.ds(pl.multiple_of(step * 8, 8), 8)
        for part in range(8 // piece):
            tile = owned[step * (8 // piece) + part]
            for column in range(KEPT):
                block[column, pl.ds(step * 8 + part * piece, piece), :] = tile[
                    :, column * rows : (column + 1) * rows
                ]

    def turn_copy(turn):
        return pltpu.make_async_remote_copy(
            src_ref=block.at[turn], dst_ref=turned.at[turn - 1],
            send_sem=turn_send.at[turn - 1], recv_sem=turn_recv.at[turn - 1],
            device_id=(place, rotated(me, turn, TA)), device_id_type=MESH,
        )

    for turn in range(1, turns + 1):
        turn_copy(turn).start()
    for column in range(KEPT):
        target = rotated(me, column, TA)
        out_ref[:, pl.ds(pl.multiple_of(target * rows, rows), rows)] = block[column]
    for turn in range(1, turns + 1):
        turn_copy(turn).wait()
        target = rotated(me, TA - turn, TA)
        out_ref[:, pl.ds(pl.multiple_of(target * rows, rows), rows)] = turned[turn - 1].T

    @pl.loop(1, groups)
    def _(step):
        target = rotated(place, step, groups)
        out_copy(place, target).wait_send()
        back_copy(place, target).wait_send()


def on_device(field, weight, coef, window_start, window_end, owner_map):
    rows = field.shape[0]
    groups = lax.axis_size("gx")
    piece = rows // groups
    total = rows * TA
    lines = jnp.transpose(field, (1, 0, 2))
    vmem = pl.BlockSpec(memory_space=pltpu.VMEM)
    smem = pl.BlockSpec(memory_space=pltpu.SMEM)
    dma = pltpu.SemaphoreType.DMA
    wide = KEPT * rows
    sums = pl.pallas_call(
        functools.partial(gram_kernel, rows, total, groups),
        out_shape=jax.ShapeDtypeStruct((3, rows, wide), jnp.float32),
        in_specs=[vmem, vmem, vmem, smem, smem],
        out_specs=vmem,
        scratch_shapes=[
            pltpu.VMEM((TA, rows, WIDTH), jnp.bfloat16),
            pltpu.VMEM((total, WIDTH), jnp.bfloat16),
            pltpu.VMEM((total, WIDTH), jnp.bfloat16),
            pltpu.VMEM((2 * BAND + 1, WIDTH), jnp.float32),
            pltpu.VMEM((1, WIDTH), jnp.float32),
            pltpu.VMEM((1, WIDTH), jnp.float32),
            pltpu.VMEM((total, PAIR * rows), jnp.float32),
            pltpu.VMEM((TA, rows, wide), jnp.float32),
            dma((CHUNKS, TA)), dma((CHUNKS, TA)), dma((CHUNKS,)),
            dma((TA,)), dma((TA,)), dma,
        ],
        compiler_params=pltpu.CompilerParams(
            collective_id=0, has_side_effects=True, vmem_limit_bytes=48 * 1024 * 1024
        ),
        name="station_gram",
    )(lines, weight[None], coef, window_start, window_end)

    turns = TA - KEPT
    owned = pl.pallas_call(
        functools.partial(owner_kernel, groups, rows),
        out_shape=jax.ShapeDtypeStruct((rows, total), jnp.float32),
        in_specs=[vmem, smem, smem, smem],
        out_specs=vmem,
        scratch_shapes=[
            pltpu.SMEM((groups,), jnp.int32),
            pltpu.VMEM((2, rows, wide), jnp.float32),
            pltpu.VMEM((groups, piece, wide), jnp.float32),
            pltpu.VMEM((groups, piece, wide), jnp.float32),
            pltpu.VMEM((groups, piece, wide), jnp.float32),
            pltpu.VMEM((groups, piece, wide), jnp.float32),
            pltpu.VMEM((KEPT, rows, rows), jnp.float32),
            pltpu.VMEM((turns, rows, rows), jnp.float32),
            dma((2,)), dma((2,)), dma((groups,)), dma((groups,)),
            dma((groups,)), dma((groups,)), dma((turns,)), dma((turns,)), dma((2,)),
        ],
        compiler_params=pltpu.CompilerParams(
            collective_id=1, has_side_effects=True, vmem_limit_bytes=32 * 1024 * 1024
        ),
        name="owner_rows",
    )(sums, window_start, window_end, owner_map)
    return owned[None]


def solution(mesh):
    placed = (P("ta", None, "gx"), P("gx"), P(), P(), P(), P())
    return jax.shard_map(
        on_device, mesh=mesh, in_specs=placed, out_specs=P("gx", "ta", None), check_vma=False
    )
```

```python
import functools

import jax
import jax.numpy as jnp
from jax import lax
from jax.experimental import pallas as pl
from jax.experimental.pallas import tpu as pltpu
from jax.sharding import PartitionSpec as P

SPAN = 8
NYW = 224
BAND = 2
STATIONS = 8
WIDTH = STATIONS * NYW
TA = 8
MESH = pl.DeviceIdType.MESH
SENT = ((0, 1), (2, 3), (4, 5), (6,), (7,))
CUTS = (0, 384, 896, 1280, 1536, 1792)
DONE = (0, 256, 896, 1152, 1408, 1792)
CHUNKS = len(SENT)
AHEAD = 2
KEPT = 5
PAIR = 6
PARTS = ((0, 3), (3, 5))


def rotated(me, step, count):
    return lax.rem(me + step, count)


def window_kernel(
    rows, total, groups, x_ref, weight_ref, coef_ref, start_ref, end_ref, owner_ref, out_ref,
    source, send, lines, scaled, taps, mean, base, gram, block, turned,
    line_send, line_recv, line_own, gram_send, gram_recv, gram_own,
    side_send, side_recv, out_send, out_recv, out_own, back_send, back_recv, back_own,
    turn_send, turn_recv, *parts,
):
    place = lax.axis_index("gx")
    me = lax.axis_index("ta")
    tall = 2 * rows
    piece = rows // groups
    turns = TA - KEPT
    landed, summed, beside, pieces, spread, ordered, owned = (
        parts[2 * kind : 2 * kind + 2] for kind in range(7)
    )

    barrier = pltpu.get_barrier_semaphore()

    @pl.loop(1, TA)
    def _(step):
        pl.semaphore_signal(
            barrier, inc=1, device_id=(place, rotated(me, step, TA)), device_id_type=MESH
        )

    @pl.loop(1, groups)
    def _(step):
        pl.semaphore_signal(
            barrier, inc=1, device_id=(rotated(place, step, groups), me), device_id_type=MESH
        )

    def line_copy(chunk, owner, target):
        lanes = slice(CUTS[chunk], CUTS[chunk + 1])
        return pltpu.make_async_remote_copy(
            src_ref=send.at[target, :, lanes],
            dst_ref=lines.at[pl.ds(pl.multiple_of(owner * rows, rows), rows), lanes],
            send_sem=line_send.at[chunk, target], recv_sem=line_recv.at[chunk, owner],
            device_id=(place, target), device_id_type=MESH,
        )

    def own_copy(chunk):
        lanes = slice(CUTS[chunk], CUTS[chunk + 1])
        return pltpu.make_async_copy(
            send.at[me, :, lanes],
            lines.at[pl.ds(pl.multiple_of(me * rows, rows), rows), lanes],
            line_own.at[chunk],
        )

    def start_lines(chunk):
        @pl.loop(1, TA)
        def _(step):
            line_copy(chunk, me, rotated(me, step, TA)).start()

    for chunk in range(CHUNKS):
        for span in SENT[chunk]:

            @pl.loop(0, rows // 16)
            def _(step):
                start = pl.multiple_of(step * 16, 16)
                tile = x_ref[span, pl.ds(start, 16), :]
                for station in range(STATIONS):
                    send[station, pl.ds(start, 16), NYW * span : NYW * (span + 1)] = tile[
                        :, NYW * station : NYW * (station + 1)
                    ]

        if chunk == 0:
            pl.semaphore_wait(barrier, TA - 1 + groups - 1)

        if chunk < AHEAD:
            start_lines(chunk)
        own_copy(chunk).start()

    weight = jnp.zeros((1, NYW), jnp.float32)
    for station in range(STATIONS):
        weight = jnp.where(
            me == station, weight_ref[:, NYW * station : NYW * (station + 1)], weight
        )
    reach = (
        lax.broadcasted_iota(jnp.int32, (2 * BAND + 1, NYW), 1)
        + lax.broadcasted_iota(jnp.int32, (2 * BAND + 1, NYW), 0) - BAND
    )
    tap = jnp.where((reach >= 0) & (reach < NYW), coef_ref[...], 0.0) * jnp.sqrt(weight)
    for span in range(SPAN):
        taps[:, NYW * span : NYW * (span + 1)] = tap

    def gram_rows(part, target):
        low, high = PARTS[part]
        begin = (lax.rem(target, 2) + low) * rows
        return gram.at[
            pl.ds(pl.multiple_of(target * rows, rows), rows),
            pl.ds(pl.multiple_of(begin, rows), (high - low) * rows),
        ]

    def gram_copy(part, owner, target):
        return pltpu.make_async_remote_copy(
            src_ref=gram_rows(part, target), dst_ref=landed[part].at[owner],
            send_sem=gram_send.at[part, target], recv_sem=gram_recv.at[part, owner],
            device_id=(place, target), device_id_type=MESH,
        )

    def gram_local(part):
        return pltpu.make_async_copy(gram_rows(part, me), landed[part].at[me], gram_own.at[part])

    def to_others(row, act):
        for side in range(2):
            target = 2 * row + side

            @pl.when(target != me)
            def _():
                act(target)

    pair = 2 * rows
    for chunk in range(CHUNKS):
        own_copy(chunk).wait()

        @pl.loop(1, TA)
        def _(step):
            line_copy(chunk, rotated(me, step, TA), me).wait_recv()

        if chunk + AHEAD < CHUNKS:

            @pl.loop(1, TA)
            def _(step):
                line_copy(chunk, me, rotated(me, step, TA)).wait_send()
            start_lines(chunk + AHEAD)

        new = slice(CUTS[chunk], CUTS[chunk + 1])
        fresh = CUTS[chunk + 1] - CUTS[chunk]

        def add(step, acc):
            start = pl.multiple_of(step * 16, 16)
            tile = lines[pl.ds(start, 16), new].astype(jnp.float32)
            return acc + tile
        acc = lax.fori_loop(0, total // 16, add, jnp.zeros((16, fresh), jnp.float32))
        mean[:, new] = jnp.sum(acc, axis=0, keepdims=True) * (1.0 / total)

        first, last = DONE[chunk], DONE[chunk + 1]
        low = first if first % (4 * NYW) == 0 else first - 128
        high = last if last % (4 * NYW) == 0 else last + 128
        lanes = slice(first, last)

        middle = slice(first - low, last - low)
        level = mean[:, low:high]
        offset_level = jnp.zeros((1, last - first), jnp.float32)
        for offset in range(2 * BAND + 1):
            moved = level if offset == BAND else pltpu.roll(level, (BAND - offset) % (high - low), 1)
            offset_level = offset_level + taps[offset : offset + 1, lanes] * moved[:, middle]
        base[:, lanes] = offset_level

        @pl.loop(0, total // tall)
        def _(step):
            at = pl.ds(pl.multiple_of(step * tall, tall), tall)
            raw = lines[at, low:high]
            filtered = taps[BAND : BAND + 1, lanes] * raw[:, middle].astype(jnp.float32)
            for offset in range(2 * BAND + 1):
                if offset != BAND:
                    moved = pltpu.roll(raw, (BAND - offset) % (high - low), 1)[:, middle]
                    filtered = filtered + taps[offset : offset + 1, lanes] * moved.astype(jnp.float32)
            scaled[at, lanes] = (filtered - base[:, lanes]).astype(jnp.bfloat16)

        def multiply(row, blocks):
            where = pl.ds(pl.multiple_of(row * pair, pair), pair)
            left = scaled[where, lanes]
            for index in blocks:
                column = lax.rem(row + index, TA // 2)
                right = scaled[pl.ds(pl.multiple_of(column * pair, pair), pair), lanes]
                product = lax.dot_general(
                    left, right, (((1,), (1,)), ((), ())), preferred_element_type=jnp.float32
                )
                at = slice(index * pair, (index + 1) * pair)
                if chunk == 0:
                    gram[where, at] = product
                else:
                    gram[where, at] = gram[where, at] + product

        if chunk < CHUNKS - 1:

            @pl.loop(0, TA // 2)
            def _(row):
                multiply(row, range(PAIR // 2))
        else:

            @pl.loop(1, TA // 2 + 1)
            def _(step):
                row = lax.rem(me // 2 + step, TA // 2)
                multiply(row, (0, 1))
                to_others(row, lambda target: gram_copy(0, me, target).start())
            gram_local(0).start()

            @pl.loop(0, TA // 2)
            def _(row):
                multiply(row, (2,))

    gram_local(1).start()

    @pl.loop(0, groups)
    def _(slot):
        window = jnp.int32(0)
        for step in range(groups):
            window = jnp.where(owner_ref[step] == slot, step, window)
        source[slot] = window
    count = ((end_ref[place] - start_ref[place]) * (SPAN * NYW)).astype(jnp.float32)

    @pl.loop(1, TA // 2 + 1)
    def _(step):
        row = lax.rem(me // 2 + step, TA // 2)

        def follow(target):
            gram_copy(0, me, target).wait_send()
            gram_copy(1, me, target).start()
        to_others(row, follow)

    next_start = jnp.where(
        place + 1 < groups, start_ref[jnp.minimum(place + 1, groups - 1)], groups * STATIONS
    )
    last_end = jnp.where(place > 0, end_ref[jnp.maximum(place - 1, 0)], 0)

    def shares(owner):
        station = place * STATIONS + owner
        upper = jnp.where(station >= next_start, 1.0, 0.0)
        lower = jnp.where(station < last_end, 1.0, 0.0)
        return upper, lower

    def reduce_part(part):
        land, total_of = landed[part], summed[part]
        gram_local(part).wait()
        upper, lower = shares(me)

        @pl.loop(0, rows // 8)
        def _(step):
            at = pl.ds(pl.multiple_of(step * 8, 8), 8)
            tile = land[me, at, :]
            total_of[0, at, :] = tile
            total_of[1, at, :] = tile * upper
            total_of[2, at, :] = tile * lower

        @pl.loop(1, TA)
        def _(count):
            owner = rotated(me, TA - count, TA)
            gram_copy(part, owner, me).wait_recv()
            upper, lower = shares(owner)

            @pl.loop(0, rows // 8)
            def _(step):
                at = pl.ds(pl.multiple_of(step * 8, 8), 8)
                tile = land[owner, at, :]
                total_of[0, at, :] = total_of[0, at, :] + tile
                total_of[1, at, :] = total_of[1, at, :] + tile * upper
                total_of[2, at, :] = total_of[2, at, :] + tile * lower

    after = rotated(place, 1, groups)
    before = rotated(place, groups - 1, groups)

    def side_copy(part, side):
        return pltpu.make_async_remote_copy(
            src_ref=summed[part].at[1 + side], dst_ref=beside[part].at[side],
            send_sem=side_send.at[part, side], recv_sem=side_recv.at[part, side],
            device_id=((after, before)[side], me), device_id_type=MESH,
        )

    def out_copy(part, owner, target):
        return pltpu.make_async_remote_copy(
            src_ref=pieces[part].at[target], dst_ref=spread[part].at[owner],
            send_sem=out_send.at[part, target], recv_sem=out_recv.at[part, owner],
            device_id=(target, me), device_id_type=MESH,
        )

    def out_local(part):
        return pltpu.make_async_copy(
            pieces[part].at[place], spread[part].at[place], out_own.at[part]
        )

    def back_copy(part, owner, target):
        return pltpu.make_async_remote_copy(
            src_ref=ordered[part].at[target], dst_ref=owned[part].at[owner],
            send_sem=back_send.at[part, target], recv_sem=back_recv.at[part, owner],
            device_id=(target, me), device_id_type=MESH,
        )

    def back_local(part):
        return pltpu.make_async_copy(
            ordered[part].at[place], owned[part].at[place], back_own.at[part]
        )

    for part in range(2):
        reduce_part(part)
        for side in range(2):
            side_copy(part, side).start()
        for side in range(2):
            side_copy(part, side).wait()

        @pl.loop(0, rows // 8)
        def _(step):
            at = pl.ds(pl.multiple_of(step * 8, 8), 8)
            tile = (summed[part][0, at, :] + beside[part][0, at, :] + beside[part][1, at, :]) / count
            for half in range(8 // piece):
                pieces[part][step * (8 // piece) + half] = tile[half * piece : (half + 1) * piece]

        @pl.loop(1, groups)
        def _(step):
            out_copy(part, place, rotated(place, step, groups)).start()
        out_local(part).start()

    for part in range(2):
        out_local(part).wait()

        @pl.loop(1, groups)
        def _(step):
            out_copy(part, rotated(place, groups - step, groups), place).wait_recv()

        @pl.loop(0, groups)
        def _(slot):
            ordered[part][slot] = spread[part][source[slot]]

        @pl.loop(1, groups)
        def _(step):
            back_copy(part, place, rotated(place, step, groups)).start()
        back_local(part).start()

    def turn_copy(turn):
        return pltpu.make_async_remote_copy(
            src_ref=block.at[turn], dst_ref=turned.at[turn - 1],
            send_sem=turn_send.at[turn - 1], recv_sem=turn_recv.at[turn - 1],
            device_id=(place, rotated(me, turn, TA)), device_id_type=MESH,
        )

    for part in range(2):
        low, high = PARTS[part]
        back_local(part).wait()

        @pl.loop(1, groups)
        def _(step):
            back_copy(part, rotated(place, groups - step, groups), place).wait_recv()

        @pl.loop(0, rows // 8)
        def _(step):
            for half in range(8 // piece):
                tile = owned[part][step * (8 // piece) + half]
                for column in range(low, high):
                    block[column, pl.ds(step * 8 + half * piece, piece), :] = tile[
                        :, (column - low) * rows : (column - low + 1) * rows
                    ]

        for column in range(low, high):
            if 1 <= column <= turns:
                turn_copy(column).start()
        for column in range(low, high):
            target = rotated(me, column, TA)
            out_ref[:, pl.ds(pl.multiple_of(target * rows, rows), rows)] = block[column]

    for turn in range(1, turns + 1):
        turn_copy(turn).wait()
        target = rotated(me, TA - turn, TA)
        out_ref[:, pl.ds(pl.multiple_of(target * rows, rows), rows)] = turned[turn - 1].T

    @pl.loop(1, TA)
    def _(step):
        target = rotated(me, step, TA)
        gram_copy(1, me, target).wait_send()
        for chunk in range(CHUNKS - AHEAD, CHUNKS):
            line_copy(chunk, me, target).wait_send()

    @pl.loop(1, groups)
    def _(step):
        target = rotated(place, step, groups)
        for part in range(2):
            out_copy(part, place, target).wait_send()
            back_copy(part, place, target).wait_send()


def on_device(field, weight, coef, window_start, window_end, owner_map):
    rows = field.shape[0]
    groups = lax.axis_size("gx")
    piece = rows // groups
    total = rows * TA
    lines = jnp.transpose(field, (1, 0, 2))
    vmem = pl.BlockSpec(memory_space=pltpu.VMEM)
    smem = pl.BlockSpec(memory_space=pltpu.SMEM)
    dma = pltpu.SemaphoreType.DMA
    turns = TA - KEPT
    widths = [(high - low) * rows for low, high in PARTS]

    def part_scratch(*shape):
        return [pltpu.VMEM((*shape, width), jnp.float32) for width in widths]

    owned = pl.pallas_call(
        functools.partial(window_kernel, rows, total, groups),
        out_shape=jax.ShapeDtypeStruct((rows, total), jnp.float32),
        in_specs=[vmem, vmem, vmem, smem, smem, smem],
        out_specs=vmem,
        scratch_shapes=[
            pltpu.SMEM((groups,), jnp.int32),
            pltpu.VMEM((TA, rows, WIDTH), jnp.bfloat16),
            pltpu.VMEM((total, WIDTH), jnp.bfloat16),
            pltpu.VMEM((total, WIDTH), jnp.bfloat16),
            pltpu.VMEM((2 * BAND + 1, WIDTH), jnp.float32),
            pltpu.VMEM((1, WIDTH), jnp.float32),
            pltpu.VMEM((1, WIDTH), jnp.float32),
            pltpu.VMEM((total, PAIR * rows), jnp.float32),
            pltpu.VMEM((KEPT, rows, rows), jnp.float32),
            pltpu.VMEM((turns, rows, rows), jnp.float32),
            dma((CHUNKS, TA)), dma((CHUNKS, TA)), dma((CHUNKS,)),
            dma((2, TA)), dma((2, TA)), dma((2,)),
            dma((2, 2)), dma((2, 2)),
            dma((2, groups)), dma((2, groups)), dma((2,)),
            dma((2, groups)), dma((2, groups)), dma((2,)),
            dma((turns,)), dma((turns,)),
            *part_scratch(TA, rows),
            *part_scratch(3, rows),
            *part_scratch(2, rows),
            *part_scratch(groups, piece),
            *part_scratch(groups, piece),
            *part_scratch(groups, piece),
            *part_scratch(groups, piece),
        ],
        compiler_params=pltpu.CompilerParams(
            collective_id=0, has_side_effects=True, vmem_limit_bytes=48 * 1024 * 1024
        ),
        name="window_rows",
    )(lines, weight[None], coef, window_start, window_end, owner_map)
    return owned[None]


def solution(mesh):
    placed = (P("ta", None, "gx"), P("gx"), P(), P(), P(), P())
    return jax.shard_map(
        on_device, mesh=mesh, in_specs=placed, out_specs=P("gx", "ta", None), check_vma=False
    )
```

```python
import functools

import jax
import jax.numpy as jnp
from jax import lax
from jax.experimental import pallas as pl
from jax.experimental.pallas import tpu as pltpu
from jax.sharding import PartitionSpec as P

SPAN = 8
NYW = 224
BAND = 2
STATIONS = 8
WIDTH = STATIONS * NYW
TA = 8
MESH = pl.DeviceIdType.MESH
SENT = ((0, 1), (2, 3), (4, 5), (6,), (7,))
CUTS = (0, 384, 896, 1280, 1536, 1792)
DONE = (0, 256, 896, 1152, 1408, 1792)
CHUNKS = len(SENT)
AHEAD = 2
KEPT = 5
PAIR = 6
PARTS = ((1, 4), (4, 5), (0, 1))
COUNT = len(PARTS)
GROUPED = ((0,), (1, 2))
TRIPS = len(GROUPED)


def rotated(me, step, count):
    return lax.rem(me + step, count)


def window_kernel(
    rows, total, groups, x_ref, weight_ref, coef_ref, start_ref, end_ref, owner_ref, out_ref,
    source, send, lines, scaled, taps, mean, base, gram, block, turned,
    line_send, line_recv, line_own, gram_send, gram_recv, gram_own,
    side_send, side_recv, out_send, out_recv, out_own, back_send, back_recv, back_own,
    turn_send, turn_recv, *parts,
):
    place = lax.axis_index("gx")
    me = lax.axis_index("ta")
    tall = 2 * rows
    tile_rows = max(rows // 2, 16)
    piece = rows // groups
    turns = TA - KEPT
    landed, summed, beside = (parts[COUNT * kind : COUNT * (kind + 1)] for kind in range(3))
    parts = parts[COUNT * 3 :]
    pieces, spread, ordered, owned = (
        parts[TRIPS * kind : TRIPS * (kind + 1)] for kind in range(4)
    )

    barrier = pltpu.get_barrier_semaphore()

    @pl.loop(1, TA)
    def _(step):
        pl.semaphore_signal(
            barrier, inc=1, device_id=(place, rotated(me, step, TA)), device_id_type=MESH
        )

    @pl.loop(1, groups)
    def _(step):
        pl.semaphore_signal(
            barrier, inc=1, device_id=(rotated(place, step, groups), me), device_id_type=MESH
        )

    def line_copy(chunk, owner, target):
        lanes = slice(CUTS[chunk], CUTS[chunk + 1])
        return pltpu.make_async_remote_copy(
            src_ref=send.at[target, :, lanes],
            dst_ref=lines.at[pl.ds(pl.multiple_of(owner * rows, rows), rows), lanes],
            send_sem=line_send.at[chunk, target], recv_sem=line_recv.at[chunk, owner],
            device_id=(place, target), device_id_type=MESH,
        )

    def own_copy(chunk):
        lanes = slice(CUTS[chunk], CUTS[chunk + 1])
        return pltpu.make_async_copy(
            send.at[me, :, lanes],
            lines.at[pl.ds(pl.multiple_of(me * rows, rows), rows), lanes],
            line_own.at[chunk],
        )

    def start_lines(chunk):
        @pl.loop(1, TA)
        def _(step):
            line_copy(chunk, me, rotated(me, step, TA)).start()

    for chunk in range(CHUNKS):
        for span in SENT[chunk]:

            @pl.loop(0, rows // tile_rows)
            def _(step):
                at = pl.ds(pl.multiple_of(step * tile_rows, tile_rows), tile_rows)
                tile = x_ref[span, at, :]
                for station in range(STATIONS):
                    send[station, at, NYW * span : NYW * (span + 1)] = tile[
                        :, NYW * station : NYW * (station + 1)
                    ]

        if chunk == 0:
            pl.semaphore_wait(barrier, TA - 1 + groups - 1)

        if chunk < AHEAD:
            start_lines(chunk)
        own_copy(chunk).start()

    for tile in range(WIDTH // 128):
        base[:, 128 * tile : 128 * (tile + 1)] = weight_ref[tile : tile + 1, :]
    weight = jnp.zeros((1, NYW), jnp.float32)
    for station in range(STATIONS):
        weight = jnp.where(
            me == station, base[:, NYW * station : NYW * (station + 1)], weight
        )
    reach = (
        lax.broadcasted_iota(jnp.int32, (2 * BAND + 1, NYW), 1)
        + lax.broadcasted_iota(jnp.int32, (2 * BAND + 1, NYW), 0) - BAND
    )
    tap = jnp.where((reach >= 0) & (reach < NYW), coef_ref[...], 0.0) * jnp.sqrt(weight)
    for span in range(SPAN):
        taps[:, NYW * span : NYW * (span + 1)] = tap

    def gram_rows(part, target):
        low, high = PARTS[part]
        begin = (lax.rem(target, 2) + low) * rows
        return gram.at[
            pl.ds(pl.multiple_of(target * rows, rows), rows),
            pl.ds(pl.multiple_of(begin, rows), (high - low) * rows),
        ]

    def gram_copy(part, owner, target):
        return pltpu.make_async_remote_copy(
            src_ref=gram_rows(part, target), dst_ref=landed[part].at[owner],
            send_sem=gram_send.at[part, target], recv_sem=gram_recv.at[part, owner],
            device_id=(place, target), device_id_type=MESH,
        )

    def gram_local(part):
        return pltpu.make_async_copy(gram_rows(part, me), landed[part].at[me], gram_own.at[part])

    def to_others(row, act):
        for side in range(2):
            target = 2 * row + side

            @pl.when(target != me)
            def _():
                act(target)

    pair = 2 * rows
    for chunk in range(CHUNKS):
        own_copy(chunk).wait()

        @pl.loop(1, TA)
        def _(step):
            line_copy(chunk, rotated(me, step, TA), me).wait_recv()

        if chunk + AHEAD < CHUNKS:

            @pl.loop(1, TA)
            def _(step):
                line_copy(chunk, me, rotated(me, step, TA)).wait_send()
            start_lines(chunk + AHEAD)

        new = slice(CUTS[chunk], CUTS[chunk + 1])
        fresh = CUTS[chunk + 1] - CUTS[chunk]

        def add(step, acc):
            start = pl.multiple_of(step * 16, 16)
            tile = lines[pl.ds(start, 16), new].astype(jnp.float32)
            return acc + tile
        acc = lax.fori_loop(0, total // 16, add, jnp.zeros((16, fresh), jnp.float32))
        mean[:, new] = jnp.sum(acc, axis=0, keepdims=True) * (1.0 / total)

        first, last = DONE[chunk], DONE[chunk + 1]
        low = first if first % (4 * NYW) == 0 else first - 128
        high = last if last % (4 * NYW) == 0 else last + 128
        lanes = slice(first, last)

        middle = slice(first - low, last - low)
        level = mean[:, low:high]
        offset_level = jnp.zeros((1, last - first), jnp.float32)
        for offset in range(2 * BAND + 1):
            moved = level if offset == BAND else pltpu.roll(level, (BAND - offset) % (high - low), 1)
            offset_level = offset_level + taps[offset : offset + 1, lanes] * moved[:, middle]
        base[:, lanes] = offset_level

        @pl.loop(0, total // tall)
        def _(step):
            at = pl.ds(pl.multiple_of(step * tall, tall), tall)
            raw = lines[at, low:high]
            filtered = taps[BAND : BAND + 1, lanes] * raw[:, middle].astype(jnp.float32)
            for offset in range(2 * BAND + 1):
                if offset != BAND:
                    moved = pltpu.roll(raw, (BAND - offset) % (high - low), 1)[:, middle]
                    filtered = filtered + taps[offset : offset + 1, lanes] * moved.astype(jnp.float32)
            scaled[at, lanes] = (filtered - base[:, lanes]).astype(jnp.bfloat16)

        def multiply(row, blocks):
            where = pl.ds(pl.multiple_of(row * pair, pair), pair)
            left = scaled[where, lanes]
            for index in blocks:
                column = lax.rem(row + index, TA // 2)
                right = scaled[pl.ds(pl.multiple_of(column * pair, pair), pair), lanes]
                product = lax.dot_general(
                    left, right, (((1,), (1,)), ((), ())), preferred_element_type=jnp.float32
                )
                at = slice(index * pair, (index + 1) * pair)
                if chunk == 0:
                    gram[where, at] = product
                else:
                    gram[where, at] = gram[where, at] + product

        if chunk < CHUNKS - 1:

            @pl.loop(0, TA // 2)
            def _(row):
                multiply(row, range(PAIR // 2))
        else:

            @pl.loop(1, TA // 2 + 1)
            def _(step):
                row = lax.rem(me // 2 + step, TA // 2)
                multiply(row, range(PAIR // 2))
                to_others(row, lambda target: gram_copy(0, me, target).start())

    for part in range(COUNT):
        gram_local(part).start()

    @pl.loop(0, groups)
    def _(slot):
        window = jnp.int32(0)
        for step in range(groups):
            window = jnp.where(owner_ref[step] == slot, step, window)
        source[slot] = window
    count = ((end_ref[place] - start_ref[place]) * (SPAN * NYW)).astype(jnp.float32)

    def follow(part):
        @pl.loop(1, TA // 2 + 1)
        def _(step):
            row = lax.rem(me // 2 + step, TA // 2)

            def act(target):
                gram_copy(part - 1, me, target).wait_send()
                gram_copy(part, me, target).start()
            to_others(row, act)

    next_start = jnp.where(
        place + 1 < groups, start_ref[jnp.minimum(place + 1, groups - 1)], groups * STATIONS
    )
    last_end = jnp.where(place > 0, end_ref[jnp.maximum(place - 1, 0)], 0)

    def shares(owner):
        station = place * STATIONS + owner
        upper = jnp.where(station >= next_start, 1.0, 0.0)
        lower = jnp.where(station < last_end, 1.0, 0.0)
        return upper, lower

    def reduce_part(part):
        land, total_of = landed[part], summed[part]
        gram_local(part).wait()
        upper, lower = shares(me)

        @pl.loop(0, rows // 8)
        def _(step):
            at = pl.ds(pl.multiple_of(step * 8, 8), 8)
            tile = land[me, at, :]
            total_of[0, at, :] = tile
            total_of[1, at, :] = tile * upper
            total_of[2, at, :] = tile * lower

        @pl.loop(1, TA)
        def _(count):
            owner = rotated(me, TA - count, TA)
            gram_copy(part, owner, me).wait_recv()
            upper, lower = shares(owner)

            @pl.loop(0, rows // 8)
            def _(step):
                at = pl.ds(pl.multiple_of(step * 8, 8), 8)
                tile = land[owner, at, :]
                total_of[0, at, :] = total_of[0, at, :] + tile
                total_of[1, at, :] = total_of[1, at, :] + tile * upper
                total_of[2, at, :] = total_of[2, at, :] + tile * lower

    after = rotated(place, 1, groups)
    before = rotated(place, groups - 1, groups)

    def side_copy(part, side):
        return pltpu.make_async_remote_copy(
            src_ref=summed[part].at[1 + side], dst_ref=beside[part].at[side],
            send_sem=side_send.at[part, side], recv_sem=side_recv.at[part, side],
            device_id=((after, before)[side], me), device_id_type=MESH,
        )

    def out_copy(part, owner, target):
        return pltpu.make_async_remote_copy(
            src_ref=pieces[part].at[target], dst_ref=spread[part].at[owner],
            send_sem=out_send.at[part, target], recv_sem=out_recv.at[part, owner],
            device_id=(target, me), device_id_type=MESH,
        )

    def out_local(part):
        return pltpu.make_async_copy(
            pieces[part].at[place], spread[part].at[place], out_own.at[part]
        )

    def back_copy(part, owner, target):
        return pltpu.make_async_remote_copy(
            src_ref=ordered[part].at[target], dst_ref=owned[part].at[owner],
            send_sem=back_send.at[part, target], recv_sem=back_recv.at[part, owner],
            device_id=(target, me), device_id_type=MESH,
        )

    def back_local(part):
        return pltpu.make_async_copy(
            ordered[part].at[place], owned[part].at[place], back_own.at[part]
        )

    def send_sides(part):
        reduce_part(part)
        for side in range(2):
            side_copy(part, side).start()

    def send_pieces(trip):
        for part in GROUPED[trip]:
            for side in range(2):
                side_copy(part, side).wait()
        scale = 1.0 / count

        @pl.loop(0, rows // 8)
        def _(step):
            at = pl.ds(pl.multiple_of(step * 8, 8), 8)
            begin = 0
            for part in GROUPED[trip]:
                tile = (
                    summed[part][0, at, :] + beside[part][0, at, :] + beside[part][1, at, :]
                ) * scale
                end = begin + tile.shape[1]
                for half in range(8 // piece):
                    pieces[trip][step * (8 // piece) + half, :, begin:end] = tile[
                        half * piece : (half + 1) * piece
                    ]
                begin = end

        @pl.loop(1, groups)
        def _(step):
            out_copy(trip, place, rotated(place, step, groups)).start()
        out_local(trip).start()

    def send_back(part):
        out_local(part).wait()

        @pl.loop(1, groups)
        def _(step):
            out_copy(part, rotated(place, groups - step, groups), place).wait_recv()

        @pl.loop(0, groups)
        def _(slot):
            ordered[part][slot] = spread[part][source[slot]]

        @pl.loop(1, groups)
        def _(step):
            back_copy(part, place, rotated(place, step, groups)).start()
        back_local(part).start()

    follow(1)
    send_sides(0)
    follow(2)
    send_sides(1)
    send_pieces(0)
    send_sides(2)
    send_pieces(1)
    for trip in range(TRIPS):
        send_back(trip)

    def turn_copy(turn):
        return pltpu.make_async_remote_copy(
            src_ref=block.at[turn], dst_ref=turned.at[turn - 1],
            send_sem=turn_send.at[turn - 1], recv_sem=turn_recv.at[turn - 1],
            device_id=(place, rotated(me, turn, TA)), device_id_type=MESH,
        )

    for trip in range(TRIPS):
        columns = [column for part in GROUPED[trip] for column in range(*PARTS[part])]
        back_local(trip).wait()

        @pl.loop(1, groups)
        def _(step):
            back_copy(trip, rotated(place, groups - step, groups), place).wait_recv()

        @pl.loop(0, rows // 8)
        def _(step):
            for half in range(8 // piece):
                tile = owned[trip][step * (8 // piece) + half]
                for slot, column in enumerate(columns):
                    block[column, pl.ds(step * 8 + half * piece, piece), :] = tile[
                        :, slot * rows : (slot + 1) * rows
                    ]

        for column in columns:
            if 1 <= column <= turns:
                turn_copy(column).start()
        for column in columns:
            target = rotated(me, column, TA)
            out_ref[:, pl.ds(pl.multiple_of(target * rows, rows), rows)] = block[column]

    for turn in range(1, turns + 1):
        turn_copy(turn).wait()
        target = rotated(me, TA - turn, TA)
        out_ref[:, pl.ds(pl.multiple_of(target * rows, rows), rows)] = turned[turn - 1].T

    @pl.loop(1, TA)
    def _(step):
        target = rotated(me, step, TA)
        gram_copy(COUNT - 1, me, target).wait_send()
        for chunk in range(CHUNKS - AHEAD, CHUNKS):
            line_copy(chunk, me, target).wait_send()

    @pl.loop(1, groups)
    def _(step):
        target = rotated(place, step, groups)
        for trip in range(TRIPS):
            out_copy(trip, place, target).wait_send()
            back_copy(trip, place, target).wait_send()


def on_device(field, weight, coef, window_start, window_end, owner_map):
    rows = field.shape[0]
    groups = lax.axis_size("gx")
    piece = rows // groups
    total = rows * TA
    lines = jnp.transpose(field, (1, 0, 2))
    vmem = pl.BlockSpec(memory_space=pltpu.VMEM)
    smem = pl.BlockSpec(memory_space=pltpu.SMEM)
    dma = pltpu.SemaphoreType.DMA
    turns = TA - KEPT
    widths = [(high - low) * rows for low, high in PARTS]
    trips = [sum(widths[part] for part in parts) for parts in GROUPED]

    def scratch(widths, *shape):
        return [pltpu.VMEM((*shape, width), jnp.float32) for width in widths]

    owned = pl.pallas_call(
        functools.partial(window_kernel, rows, total, groups),
        out_shape=jax.ShapeDtypeStruct((rows, total), jnp.float32),
        in_specs=[vmem, vmem, vmem, smem, smem, smem],
        out_specs=vmem,
        scratch_shapes=[
            pltpu.SMEM((groups,), jnp.int32),
            pltpu.VMEM((TA, rows, WIDTH), jnp.bfloat16),
            pltpu.VMEM((total, WIDTH), jnp.bfloat16),
            pltpu.VMEM((total, WIDTH), jnp.bfloat16),
            pltpu.VMEM((2 * BAND + 1, WIDTH), jnp.float32),
            pltpu.VMEM((1, WIDTH), jnp.float32),
            pltpu.VMEM((1, WIDTH), jnp.float32),
            pltpu.VMEM((total, PAIR * rows), jnp.float32),
            pltpu.VMEM((KEPT, rows, rows), jnp.float32),
            pltpu.VMEM((turns, rows, rows), jnp.float32),
            dma((CHUNKS, TA)), dma((CHUNKS, TA)), dma((CHUNKS,)),
            dma((COUNT, TA)), dma((COUNT, TA)), dma((COUNT,)),
            dma((COUNT, 2)), dma((COUNT, 2)),
            dma((TRIPS, groups)), dma((TRIPS, groups)), dma((TRIPS,)),
            dma((TRIPS, groups)), dma((TRIPS, groups)), dma((TRIPS,)),
            dma((turns,)), dma((turns,)),
            *scratch(widths, TA, rows),
            *scratch(widths, 3, rows),
            *scratch(widths, 2, rows),
            *scratch(trips, groups, piece),
            *scratch(trips, groups, piece),
            *scratch(trips, groups, piece),
            *scratch(trips, groups, piece),
        ],
        compiler_params=pltpu.CompilerParams(
            collective_id=0, has_side_effects=True, vmem_limit_bytes=48 * 1024 * 1024
        ),
        name="window_rows",
    )(lines, weight.reshape(WIDTH // 128, 128), coef, window_start, window_end, owner_map)
    return owned[None]


def solution(mesh):
    placed = (P("ta", None, "gx"), P("gx"), P(), P(), P(), P())
    return jax.shard_map(
        on_device, mesh=mesh, in_specs=placed, out_specs=P("gx", "ta", None), check_vma=False
    )
```

```python
import functools

import jax
import jax.numpy as jnp
from jax import lax
from jax.experimental import pallas as pl
from jax.experimental.pallas import tpu as pltpu
from jax.sharding import PartitionSpec as P

SPAN = 8
NYW = 224
BAND = 2
STATIONS = 8
WIDTH = STATIONS * NYW
TA = 8
MESH = pl.DeviceIdType.MESH
SENT = ((0, 1), (2, 3), (4, 5), (6,), (7,))
CUTS = (0, 384, 896, 1280, 1536, 1792)
DONE = (0, 256, 896, 1152, 1408, 1792)
CHUNKS = len(SENT)
AHEAD = 2
KEPT = 5
PAIR = 6
PARTS = ((1, 4), (4, 5), (0, 1))
COUNT = len(PARTS)
GROUPED = ((0,), (1, 2))
TRIPS = len(GROUPED)


def rotated(me, step, count):
    return lax.rem(me + step, count)


def window_kernel(
    rows, total, groups, x_ref, weight_ref, coef_ref, start_ref, end_ref, owner_ref, out_ref,
    source, send, lines, scaled, taps, mean, base, gram, block, turned,
    line_send, line_recv, line_own, gram_send, gram_recv, gram_own,
    side_send, side_recv, out_send, out_recv, out_own, back_send, back_recv, back_own,
    turn_send, turn_recv, *parts,
):
    place = lax.axis_index("gx")
    me = lax.axis_index("ta")
    tall = 2 * rows
    tile_rows = max(rows // 2, 16)
    piece = rows // groups
    turns = TA - KEPT
    landed, summed, beside = (parts[COUNT * kind : COUNT * (kind + 1)] for kind in range(3))
    parts = parts[COUNT * 3 :]
    pieces, spread, ordered, owned = (
        parts[TRIPS * kind : TRIPS * (kind + 1)] for kind in range(4)
    )

    barrier = pltpu.get_barrier_semaphore()

    @pl.loop(1, TA)
    def _(step):
        pl.semaphore_signal(
            barrier, inc=1, device_id=(place, rotated(me, step, TA)), device_id_type=MESH
        )

    @pl.loop(1, groups)
    def _(step):
        pl.semaphore_signal(
            barrier, inc=1, device_id=(rotated(place, step, groups), me), device_id_type=MESH
        )

    def line_copy(chunk, owner, target):
        lanes = slice(CUTS[chunk], CUTS[chunk + 1])
        return pltpu.make_async_remote_copy(
            src_ref=send.at[target, :, lanes],
            dst_ref=lines.at[pl.ds(pl.multiple_of(owner * rows, rows), rows), lanes],
            send_sem=line_send.at[chunk, target], recv_sem=line_recv.at[chunk, owner],
            device_id=(place, target), device_id_type=MESH,
        )

    def own_copy(chunk):
        lanes = slice(CUTS[chunk], CUTS[chunk + 1])
        return pltpu.make_async_copy(
            send.at[me, :, lanes],
            lines.at[pl.ds(pl.multiple_of(me * rows, rows), rows), lanes],
            line_own.at[chunk],
        )

    def start_lines(chunk):
        @pl.loop(1, TA)
        def _(step):
            line_copy(chunk, me, rotated(me, step, TA)).start()

    for chunk in range(CHUNKS):
        for span in SENT[chunk]:

            @pl.loop(0, rows // tile_rows)
            def _(step):
                at = pl.ds(pl.multiple_of(step * tile_rows, tile_rows), tile_rows)
                tile = x_ref[span, at, :]
                for station in range(STATIONS):
                    send[station, at, NYW * span : NYW * (span + 1)] = tile[
                        :, NYW * station : NYW * (station + 1)
                    ]

        if chunk == 0:
            pl.semaphore_wait(barrier, TA - 1 + groups - 1)

        if chunk < AHEAD:
            start_lines(chunk)
        own_copy(chunk).start()

    for tile in range(WIDTH // 128):
        base[:, 128 * tile : 128 * (tile + 1)] = weight_ref[tile : tile + 1, :]
    weight = jnp.zeros((1, NYW), jnp.float32)
    for station in range(STATIONS):
        weight = jnp.where(
            me == station, base[:, NYW * station : NYW * (station + 1)], weight
        )
    reach = (
        lax.broadcasted_iota(jnp.int32, (2 * BAND + 1, NYW), 1)
        + lax.broadcasted_iota(jnp.int32, (2 * BAND + 1, NYW), 0) - BAND
    )
    tap = jnp.where((reach >= 0) & (reach < NYW), coef_ref[...], 0.0) * jnp.sqrt(weight)
    for span in range(SPAN):
        taps[:, NYW * span : NYW * (span + 1)] = tap

    def gram_rows(part, target):
        low, high = PARTS[part]
        begin = (lax.rem(target, 2) + low) * rows
        return gram.at[
            pl.ds(pl.multiple_of(target * rows, rows), rows),
            pl.ds(pl.multiple_of(begin, rows), (high - low) * rows),
        ]

    def gram_copy(part, owner, target):
        return pltpu.make_async_remote_copy(
            src_ref=gram_rows(part, target), dst_ref=landed[part].at[owner],
            send_sem=gram_send.at[part, target], recv_sem=gram_recv.at[part, owner],
            device_id=(place, target), device_id_type=MESH,
        )

    def gram_local(part):
        return pltpu.make_async_copy(gram_rows(part, me), landed[part].at[me], gram_own.at[part])

    def to_others(row, act):
        for side in range(2):
            target = 2 * row + side

            @pl.when(target != me)
            def _():
                act(target)

    pair = 2 * rows
    for chunk in range(CHUNKS):
        own_copy(chunk).wait()

        @pl.loop(1, TA)
        def _(step):
            line_copy(chunk, rotated(me, step, TA), me).wait_recv()

        if chunk + AHEAD < CHUNKS:

            @pl.loop(1, TA)
            def _(step):
                line_copy(chunk, me, rotated(me, step, TA)).wait_send()
            start_lines(chunk + AHEAD)

        new = slice(CUTS[chunk], CUTS[chunk + 1])
        fresh = CUTS[chunk + 1] - CUTS[chunk]

        def add(step, acc):
            start = pl.multiple_of(step * 16, 16)
            tile = lines[pl.ds(start, 16), new].astype(jnp.float32)
            return acc + tile
        acc = lax.fori_loop(0, total // 16, add, jnp.zeros((16, fresh), jnp.float32))
        mean[:, new] = jnp.sum(acc, axis=0, keepdims=True) * (1.0 / total)

        first, last = DONE[chunk], DONE[chunk + 1]
        low = first if first % (4 * NYW) == 0 else first - 128
        high = last if last % (4 * NYW) == 0 else last + 128
        lanes = slice(first, last)

        middle = slice(first - low, last - low)
        level = mean[:, low:high]
        offset_level = jnp.zeros((1, last - first), jnp.float32)
        for offset in range(2 * BAND + 1):
            moved = level if offset == BAND else pltpu.roll(level, (BAND - offset) % (high - low), 1)
            offset_level = offset_level + taps[offset : offset + 1, lanes] * moved[:, middle]
        base[:, lanes] = offset_level

        @pl.loop(0, total // tall)
        def _(step):
            at = pl.ds(pl.multiple_of(step * tall, tall), tall)
            raw = lines[at, low:high]
            filtered = taps[BAND : BAND + 1, lanes] * raw[:, middle].astype(jnp.float32)
            for offset in range(2 * BAND + 1):
                if offset != BAND:
                    moved = pltpu.roll(raw, (BAND - offset) % (high - low), 1)[:, middle]
                    filtered = filtered + taps[offset : offset + 1, lanes] * moved.astype(jnp.float32)
            scaled[at, lanes] = (filtered - base[:, lanes]).astype(jnp.bfloat16)

        def multiply(row, blocks):
            where = pl.ds(pl.multiple_of(row * pair, pair), pair)
            left = scaled[where, lanes]
            for index in blocks:
                column = lax.rem(row + index, TA // 2)
                right = scaled[pl.ds(pl.multiple_of(column * pair, pair), pair), lanes]
                product = lax.dot_general(
                    left, right, (((1,), (1,)), ((), ())), preferred_element_type=jnp.float32
                )
                at = slice(index * pair, (index + 1) * pair)
                if chunk == 0:
                    gram[where, at] = product
                else:
                    gram[where, at] = gram[where, at] + product

        if chunk < CHUNKS - 1:

            @pl.loop(0, TA // 2)
            def _(row):
                multiply(row, range(PAIR // 2))
        else:

            @pl.loop(1, TA // 2 + 1)
            def _(step):
                row = lax.rem(me // 2 + step, TA // 2)
                multiply(row, range(PAIR // 2))
                to_others(row, lambda target: gram_copy(0, me, target).start())

    for part in range(COUNT):
        gram_local(part).start()

    @pl.loop(0, groups)
    def _(slot):
        window = jnp.int32(0)
        for step in range(groups):
            window = jnp.where(owner_ref[step] == slot, step, window)
        source[slot] = window
    count = ((end_ref[place] - start_ref[place]) * (SPAN * NYW)).astype(jnp.float32)

    def follow(part):
        @pl.loop(1, TA // 2 + 1)
        def _(step):
            row = lax.rem(me // 2 + step, TA // 2)

            def act(target):
                gram_copy(part - 1, me, target).wait_send()
                gram_copy(part, me, target).start()
            to_others(row, act)

    next_start = jnp.where(
        place + 1 < groups, start_ref[jnp.minimum(place + 1, groups - 1)], groups * STATIONS
    )
    last_end = jnp.where(place > 0, end_ref[jnp.maximum(place - 1, 0)], 0)

    def shares(owner):
        station = place * STATIONS + owner
        upper = jnp.where(station >= next_start, 1.0, 0.0)
        lower = jnp.where(station < last_end, 1.0, 0.0)
        return upper, lower

    def reduce_part(part):
        land, total_of = landed[part], summed[part]
        gram_local(part).wait()
        upper, lower = shares(me)

        @pl.loop(0, rows // 8)
        def _(step):
            at = pl.ds(pl.multiple_of(step * 8, 8), 8)
            tile = land[me, at, :]
            total_of[0, at, :] = tile
            total_of[1, at, :] = tile * upper
            total_of[2, at, :] = tile * lower

        @pl.loop(1, TA)
        def _(count):
            owner = rotated(me, TA - count, TA)
            gram_copy(part, owner, me).wait_recv()
            upper, lower = shares(owner)

            @pl.loop(0, rows // 8)
            def _(step):
                at = pl.ds(pl.multiple_of(step * 8, 8), 8)
                tile = land[owner, at, :]
                total_of[0, at, :] = total_of[0, at, :] + tile
                total_of[1, at, :] = total_of[1, at, :] + tile * upper
                total_of[2, at, :] = total_of[2, at, :] + tile * lower

    after = rotated(place, 1, groups)
    before = rotated(place, groups - 1, groups)

    def side_copy(part, side):
        return pltpu.make_async_remote_copy(
            src_ref=summed[part].at[1 + side], dst_ref=beside[part].at[side],
            send_sem=side_send.at[part, side], recv_sem=side_recv.at[part, side],
            device_id=((after, before)[side], me), device_id_type=MESH,
        )

    def out_copy(part, owner, target):
        return pltpu.make_async_remote_copy(
            src_ref=pieces[part].at[target], dst_ref=spread[part].at[owner],
            send_sem=out_send.at[part], recv_sem=out_recv.at[part],
            device_id=(target, me), device_id_type=MESH,
        )

    def out_all(part):
        return pltpu.make_async_remote_copy(
            src_ref=pieces[part].at[: groups - 1], dst_ref=spread[part].at[: groups - 1],
            send_sem=out_send.at[part], recv_sem=out_recv.at[part],
            device_id=(place, me), device_id_type=MESH,
        )

    def back_all(part):
        return pltpu.make_async_remote_copy(
            src_ref=ordered[part].at[: groups - 1], dst_ref=owned[part].at[: groups - 1],
            send_sem=back_send.at[part], recv_sem=back_recv.at[part],
            device_id=(place, me), device_id_type=MESH,
        )

    def out_local(part):
        return pltpu.make_async_copy(
            pieces[part].at[place], spread[part].at[place], out_own.at[part]
        )

    def back_copy(part, owner, target):
        return pltpu.make_async_remote_copy(
            src_ref=ordered[part].at[target], dst_ref=owned[part].at[owner],
            send_sem=back_send.at[part], recv_sem=back_recv.at[part],
            device_id=(target, me), device_id_type=MESH,
        )

    def back_local(part):
        return pltpu.make_async_copy(
            ordered[part].at[place], owned[part].at[place], back_own.at[part]
        )

    def send_sides(part):
        reduce_part(part)
        for side in range(2):
            side_copy(part, side).start()

    def send_pieces(trip):
        for part in GROUPED[trip]:
            for side in range(2):
                side_copy(part, side).wait()
        scale = 1.0 / count

        @pl.loop(0, rows // 8)
        def _(step):
            at = pl.ds(pl.multiple_of(step * 8, 8), 8)
            begin = 0
            for part in GROUPED[trip]:
                tile = (
                    summed[part][0, at, :] + beside[part][0, at, :] + beside[part][1, at, :]
                ) * scale
                end = begin + tile.shape[1]
                for half in range(8 // piece):
                    pieces[trip][step * (8 // piece) + half, :, begin:end] = tile[
                        half * piece : (half + 1) * piece
                    ]
                begin = end

        @pl.loop(1, groups)
        def _(step):
            out_copy(trip, place, rotated(place, step, groups)).start()
        out_local(trip).start()

    def send_back(part):
        out_local(part).wait()

        out_all(part).wait_recv()

        @pl.loop(0, groups)
        def _(slot):
            ordered[part][slot] = spread[part][source[slot]]

        @pl.loop(1, groups)
        def _(step):
            back_copy(part, place, rotated(place, step, groups)).start()
        back_local(part).start()

    follow(1)
    send_sides(0)
    follow(2)
    send_sides(1)
    send_pieces(0)
    send_sides(2)
    send_pieces(1)
    for trip in range(TRIPS):
        send_back(trip)

    def turn_copy(turn):
        return pltpu.make_async_remote_copy(
            src_ref=block.at[turn], dst_ref=turned.at[turn - 1],
            send_sem=turn_send.at[turn - 1], recv_sem=turn_recv.at[turn - 1],
            device_id=(place, rotated(me, turn, TA)), device_id_type=MESH,
        )

    @pl.loop(1, TA)
    def _(step):
        target = rotated(me, step, TA)
        gram_copy(COUNT - 1, me, target).wait_send()
        for chunk in range(CHUNKS - AHEAD, CHUNKS):
            line_copy(chunk, me, target).wait_send()

    for trip in range(TRIPS):
        out_all(trip).wait_send()
        back_all(trip).wait_send()

    for trip in range(TRIPS):
        columns = [column for part in GROUPED[trip] for column in range(*PARTS[part])]
        back_local(trip).wait()

        back_all(trip).wait_recv()

        @pl.loop(0, rows // 8)
        def _(step):
            for half in range(8 // piece):
                tile = owned[trip][step * (8 // piece) + half]
                for slot, column in enumerate(columns):
                    block[column, pl.ds(step * 8 + half * piece, piece), :] = tile[
                        :, slot * rows : (slot + 1) * rows
                    ]

        for column in columns:
            if 1 <= column <= turns:
                turn_copy(column).start()
        for column in columns:
            target = rotated(me, column, TA)
            out_ref[:, pl.ds(pl.multiple_of(target * rows, rows), rows)] = block[column]

    for turn in range(1, turns + 1):
        turn_copy(turn).wait()
        target = rotated(me, TA - turn, TA)
        out_ref[:, pl.ds(pl.multiple_of(target * rows, rows), rows)] = turned[turn - 1].T


def on_device(field, weight, coef, window_start, window_end, owner_map):
    rows = field.shape[0]
    groups = lax.axis_size("gx")
    piece = rows // groups
    total = rows * TA
    lines = jnp.transpose(field, (1, 0, 2))
    vmem = pl.BlockSpec(memory_space=pltpu.VMEM)
    smem = pl.BlockSpec(memory_space=pltpu.SMEM)
    dma = pltpu.SemaphoreType.DMA
    turns = TA - KEPT
    widths = [(high - low) * rows for low, high in PARTS]
    trips = [sum(widths[part] for part in parts) for parts in GROUPED]

    def scratch(widths, *shape):
        return [pltpu.VMEM((*shape, width), jnp.float32) for width in widths]

    owned = pl.pallas_call(
        functools.partial(window_kernel, rows, total, groups),
        out_shape=jax.ShapeDtypeStruct((rows, total), jnp.float32),
        in_specs=[vmem, vmem, vmem, smem, smem, smem],
        out_specs=vmem,
        scratch_shapes=[
            pltpu.SMEM((groups,), jnp.int32),
            pltpu.VMEM((TA, rows, WIDTH), jnp.bfloat16),
            pltpu.VMEM((total, WIDTH), jnp.bfloat16),
            pltpu.VMEM((total, WIDTH), jnp.bfloat16),
            pltpu.VMEM((2 * BAND + 1, WIDTH), jnp.float32),
            pltpu.VMEM((1, WIDTH), jnp.float32),
            pltpu.VMEM((1, WIDTH), jnp.float32),
            pltpu.VMEM((total, PAIR * rows), jnp.float32),
            pltpu.VMEM((KEPT, rows, rows), jnp.float32),
            pltpu.VMEM((turns, rows, rows), jnp.float32),
            dma((CHUNKS, TA)), dma((CHUNKS, TA)), dma((CHUNKS,)),
            dma((COUNT, TA)), dma((COUNT, TA)), dma((COUNT,)),
            dma((COUNT, 2)), dma((COUNT, 2)),
            dma((TRIPS,)), dma((TRIPS,)), dma((TRIPS,)),
            dma((TRIPS,)), dma((TRIPS,)), dma((TRIPS,)),
            dma((turns,)), dma((turns,)),
            *scratch(widths, TA, rows),
            *scratch(widths, 3, rows),
            *scratch(widths, 2, rows),
            *scratch(trips, groups, piece),
            *scratch(trips, groups, piece),
            *scratch(trips, groups, piece),
            *scratch(trips, groups, piece),
        ],
        compiler_params=pltpu.CompilerParams(
            collective_id=0, has_side_effects=True, vmem_limit_bytes=48 * 1024 * 1024
        ),
        name="window_rows",
    )(lines, weight.reshape(WIDTH // 128, 128), coef, window_start, window_end, owner_map)
    return owned[None]


def solution(mesh):
    placed = (P("ta", None, "gx"), P("gx"), P(), P(), P(), P())
    return jax.shard_map(
        on_device, mesh=mesh, in_specs=placed, out_specs=P("gx", "ta", None), check_vma=False
    )
```

```python
import functools

import jax
import jax.numpy as jnp
from jax import lax
from jax.experimental import pallas as pl
from jax.experimental.pallas import tpu as pltpu
from jax.sharding import PartitionSpec as P

SPAN = 8
NYW = 224
BAND = 2
STATIONS = 8
WIDTH = STATIONS * NYW
TA = 8
MESH = pl.DeviceIdType.MESH
SENT = ((0, 1), (2, 3), (4, 5), (6,), (7,))
CUTS = (0, 384, 896, 1280, 1536, 1792)
DONE = (0, 256, 896, 1152, 1408, 1792)
CHUNKS = len(SENT)
AHEAD = 2
KEPT = 5
PAIR = 6
PARTS = ((1, 4), (4, 5), (0, 1))
COUNT = len(PARTS)
GROUPED = ((0,), (1, 2))
TRIPS = len(GROUPED)


def rotated(me, step, count):
    return lax.rem(me + step, count)


def window_kernel(
    rows, total, groups, x_ref, weight_ref, coef_ref, start_ref, end_ref, owner_ref, out_ref,
    source, send, lines, scaled, taps, mean, base, gram, block, turned,
    line_send, line_recv, line_own, gram_send, gram_recv, gram_own,
    side_send, side_recv, out_send, out_recv, out_own, back_send, back_recv, back_own,
    turn_send, turn_recv, *parts,
):
    place = lax.axis_index("gx")
    me = lax.axis_index("ta")
    tall = 2 * rows
    tile_rows = max(rows // 2, 16)
    piece = rows // groups
    turns = TA - KEPT
    landed, summed, beside = (parts[COUNT * kind : COUNT * (kind + 1)] for kind in range(3))
    parts = parts[COUNT * 3 :]
    pieces, spread, ordered, owned = (
        parts[TRIPS * kind : TRIPS * (kind + 1)] for kind in range(4)
    )

    barrier = pltpu.get_barrier_semaphore()

    @pl.loop(1, TA)
    def _(step):
        pl.semaphore_signal(
            barrier, inc=1, device_id=(place, rotated(me, step, TA)), device_id_type=MESH
        )

    @pl.loop(1, groups)
    def _(step):
        pl.semaphore_signal(
            barrier, inc=1, device_id=(rotated(place, step, groups), me), device_id_type=MESH
        )

    def line_copy(chunk, owner, target):
        lanes = slice(CUTS[chunk], CUTS[chunk + 1])
        return pltpu.make_async_remote_copy(
            src_ref=send.at[target, :, lanes],
            dst_ref=lines.at[pl.ds(pl.multiple_of(owner * rows, rows), rows), lanes],
            send_sem=line_send.at[chunk], recv_sem=line_recv.at[chunk],
            device_id=(place, target), device_id_type=MESH,
        )

    def all_lines(chunk):
        lanes = slice(CUTS[chunk], CUTS[chunk + 1])
        some = lines.at[: (TA - 1) * rows, lanes]
        return pltpu.make_async_remote_copy(
            src_ref=some, dst_ref=some,
            send_sem=line_send.at[chunk], recv_sem=line_recv.at[chunk],
            device_id=(place, me), device_id_type=MESH,
        )

    def own_copy(chunk):
        lanes = slice(CUTS[chunk], CUTS[chunk + 1])
        return pltpu.make_async_copy(
            send.at[me, :, lanes],
            lines.at[pl.ds(pl.multiple_of(me * rows, rows), rows), lanes],
            line_own.at[chunk],
        )

    def start_lines(chunk):
        @pl.loop(1, TA)
        def _(step):
            line_copy(chunk, me, rotated(me, step, TA)).start()

    for chunk in range(CHUNKS):
        for span in SENT[chunk]:

            @pl.loop(0, rows // tile_rows)
            def _(step):
                at = pl.ds(pl.multiple_of(step * tile_rows, tile_rows), tile_rows)
                tile = x_ref[span, at, :]
                for station in range(STATIONS):
                    send[station, at, NYW * span : NYW * (span + 1)] = tile[
                        :, NYW * station : NYW * (station + 1)
                    ]

        if chunk == 0:
            pl.semaphore_wait(barrier, TA - 1 + groups - 1)

        if chunk < AHEAD:
            start_lines(chunk)
        own_copy(chunk).start()

    for tile in range(WIDTH // 128):
        base[:, 128 * tile : 128 * (tile + 1)] = weight_ref[tile : tile + 1, :]
    weight = jnp.zeros((1, NYW), jnp.float32)
    for station in range(STATIONS):
        weight = jnp.where(
            me == station, base[:, NYW * station : NYW * (station + 1)], weight
        )
    reach = (
        lax.broadcasted_iota(jnp.int32, (2 * BAND + 1, NYW), 1)
        + lax.broadcasted_iota(jnp.int32, (2 * BAND + 1, NYW), 0) - BAND
    )
    tap = jnp.where((reach >= 0) & (reach < NYW), coef_ref[...], 0.0) * jnp.sqrt(weight)
    for span in range(SPAN):
        taps[:, NYW * span : NYW * (span + 1)] = tap

    def gram_rows(part, target):
        low, high = PARTS[part]
        begin = (lax.rem(target, 2) + low) * rows
        return gram.at[
            pl.ds(pl.multiple_of(target * rows, rows), rows),
            pl.ds(pl.multiple_of(begin, rows), (high - low) * rows),
        ]

    def gram_copy(part, owner, target):
        return pltpu.make_async_remote_copy(
            src_ref=gram_rows(part, target), dst_ref=landed[part].at[owner],
            send_sem=gram_send.at[part, target], recv_sem=gram_recv.at[part, owner],
            device_id=(place, target), device_id_type=MESH,
        )

    def gram_local(part):
        return pltpu.make_async_copy(gram_rows(part, me), landed[part].at[me], gram_own.at[part])

    def to_others(row, act):
        for side in range(2):
            target = 2 * row + side

            @pl.when(target != me)
            def _():
                act(target)

    pair = 2 * rows
    for chunk in range(CHUNKS):
        own_copy(chunk).wait()

        all_lines(chunk).wait_recv()

        if chunk + AHEAD < CHUNKS:
            all_lines(chunk).wait_send()
            start_lines(chunk + AHEAD)

        new = slice(CUTS[chunk], CUTS[chunk + 1])
        fresh = CUTS[chunk + 1] - CUTS[chunk]

        def add(step, acc):
            start = pl.multiple_of(step * 16, 16)
            tile = lines[pl.ds(start, 16), new].astype(jnp.float32)
            return acc + tile
        acc = lax.fori_loop(0, total // 16, add, jnp.zeros((16, fresh), jnp.float32), unroll=4)
        mean[:, new] = jnp.sum(acc, axis=0, keepdims=True) * (1.0 / total)

        first, last = DONE[chunk], DONE[chunk + 1]
        low = first if first % (4 * NYW) == 0 else first - 128
        high = last if last % (4 * NYW) == 0 else last + 128
        lanes = slice(first, last)

        middle = slice(first - low, last - low)
        level = mean[:, low:high]
        offset_level = jnp.zeros((1, last - first), jnp.float32)
        for offset in range(2 * BAND + 1):
            moved = level if offset == BAND else pltpu.roll(level, (BAND - offset) % (high - low), 1)
            offset_level = offset_level + taps[offset : offset + 1, lanes] * moved[:, middle]
        base[:, lanes] = offset_level

        @pl.loop(0, total // tall)
        def _(step):
            at = pl.ds(pl.multiple_of(step * tall, tall), tall)
            raw = lines[at, low:high]
            filtered = taps[BAND : BAND + 1, lanes] * raw[:, middle].astype(jnp.float32)
            for offset in range(2 * BAND + 1):
                if offset != BAND:
                    moved = pltpu.roll(raw, (BAND - offset) % (high - low), 1)[:, middle]
                    filtered = filtered + taps[offset : offset + 1, lanes] * moved.astype(jnp.float32)
            scaled[at, lanes] = (filtered - base[:, lanes]).astype(jnp.bfloat16)

        def multiply(row, blocks):
            where = pl.ds(pl.multiple_of(row * pair, pair), pair)
            left = scaled[where, lanes]
            for index in blocks:
                column = lax.rem(row + index, TA // 2)
                right = scaled[pl.ds(pl.multiple_of(column * pair, pair), pair), lanes]
                product = lax.dot_general(
                    left, right, (((1,), (1,)), ((), ())), preferred_element_type=jnp.float32
                )
                at = slice(index * pair, (index + 1) * pair)
                if chunk == 0:
                    gram[where, at] = product
                else:
                    gram[where, at] = gram[where, at] + product

        if chunk < CHUNKS - 1:

            @pl.loop(0, TA // 2)
            def _(row):
                multiply(row, range(PAIR // 2))
        else:

            @pl.loop(1, TA // 2 + 1)
            def _(step):
                row = lax.rem(me // 2 + step, TA // 2)
                multiply(row, range(PAIR // 2))
                to_others(row, lambda target: gram_copy(0, me, target).start())

    for part in range(COUNT):
        gram_local(part).start()

    @pl.loop(0, groups)
    def _(slot):
        window = jnp.int32(0)
        for step in range(groups):
            window = jnp.where(owner_ref[step] == slot, step, window)
        source[slot] = window
    count = ((end_ref[place] - start_ref[place]) * (SPAN * NYW)).astype(jnp.float32)

    def follow(part):
        @pl.loop(1, TA // 2 + 1)
        def _(step):
            row = lax.rem(me // 2 + step, TA // 2)

            def act(target):
                gram_copy(part - 1, me, target).wait_send()
                gram_copy(part, me, target).start()
            to_others(row, act)

    next_start = jnp.where(
        place + 1 < groups, start_ref[jnp.minimum(place + 1, groups - 1)], groups * STATIONS
    )
    last_end = jnp.where(place > 0, end_ref[jnp.maximum(place - 1, 0)], 0)

    def shares(owner):
        station = place * STATIONS + owner
        upper = jnp.where(station >= next_start, 1.0, 0.0)
        lower = jnp.where(station < last_end, 1.0, 0.0)
        return upper, lower

    def reduce_part(part):
        land, total_of = landed[part], summed[part]
        gram_local(part).wait()
        upper, lower = shares(me)

        @pl.loop(0, rows // 8)
        def _(step):
            at = pl.ds(pl.multiple_of(step * 8, 8), 8)
            tile = land[me, at, :]
            total_of[0, at, :] = tile
            total_of[1, at, :] = tile * upper
            total_of[2, at, :] = tile * lower

        @pl.loop(1, TA)
        def _(count):
            owner = rotated(me, TA - count, TA)
            gram_copy(part, owner, me).wait_recv()
            upper, lower = shares(owner)

            @pl.loop(0, rows // 8)
            def _(step):
                at = pl.ds(pl.multiple_of(step * 8, 8), 8)
                tile = land[owner, at, :]
                total_of[0, at, :] = total_of[0, at, :] + tile
                total_of[1, at, :] = total_of[1, at, :] + tile * upper
                total_of[2, at, :] = total_of[2, at, :] + tile * lower

    after = rotated(place, 1, groups)
    before = rotated(place, groups - 1, groups)

    def side_copy(part, side):
        return pltpu.make_async_remote_copy(
            src_ref=summed[part].at[1 + side], dst_ref=beside[part].at[side],
            send_sem=side_send.at[part, side], recv_sem=side_recv.at[part, side],
            device_id=((after, before)[side], me), device_id_type=MESH,
        )

    def out_copy(part, owner, target):
        return pltpu.make_async_remote_copy(
            src_ref=pieces[part].at[target], dst_ref=spread[part].at[owner],
            send_sem=out_send.at[part], recv_sem=out_recv.at[part],
            device_id=(target, me), device_id_type=MESH,
        )

    def out_all(part):
        return pltpu.make_async_remote_copy(
            src_ref=pieces[part].at[: groups - 1], dst_ref=spread[part].at[: groups - 1],
            send_sem=out_send.at[part], recv_sem=out_recv.at[part],
            device_id=(place, me), device_id_type=MESH,
        )

    def back_all(part):
        return pltpu.make_async_remote_copy(
            src_ref=ordered[part].at[: groups - 1], dst_ref=owned[part].at[: groups - 1],
            send_sem=back_send.at[part], recv_sem=back_recv.at[part],
            device_id=(place, me), device_id_type=MESH,
        )

    def out_local(part):
        return pltpu.make_async_copy(
            pieces[part].at[place], spread[part].at[place], out_own.at[part]
        )

    def back_copy(part, owner, target):
        return pltpu.make_async_remote_copy(
            src_ref=ordered[part].at[target], dst_ref=owned[part].at[owner],
            send_sem=back_send.at[part], recv_sem=back_recv.at[part],
            device_id=(target, me), device_id_type=MESH,
        )

    def back_local(part):
        return pltpu.make_async_copy(
            ordered[part].at[place], owned[part].at[place], back_own.at[part]
        )

    def send_sides(part):
        reduce_part(part)
        for side in range(2):
            side_copy(part, side).start()

    def send_pieces(trip):
        for part in GROUPED[trip]:
            for side in range(2):
                side_copy(part, side).wait()
        scale = 1.0 / count

        @pl.loop(0, rows // 8)
        def _(step):
            at = pl.ds(pl.multiple_of(step * 8, 8), 8)
            begin = 0
            for part in GROUPED[trip]:
                tile = (
                    summed[part][0, at, :] + beside[part][0, at, :] + beside[part][1, at, :]
                ) * scale
                end = begin + tile.shape[1]
                for half in range(8 // piece):
                    pieces[trip][step * (8 // piece) + half, :, begin:end] = tile[
                        half * piece : (half + 1) * piece
                    ]
                begin = end

        @pl.loop(1, groups)
        def _(step):
            out_copy(trip, place, rotated(place, step, groups)).start()
        out_local(trip).start()

    def send_back(part):
        out_local(part).wait()

        out_all(part).wait_recv()

        @pl.loop(0, groups)
        def _(slot):
            ordered[part][slot] = spread[part][source[slot]]

        @pl.loop(1, groups)
        def _(step):
            back_copy(part, place, rotated(place, step, groups)).start()
        back_local(part).start()

    follow(1)
    send_sides(0)
    follow(2)
    send_sides(1)
    send_pieces(0)
    send_sides(2)
    send_pieces(1)
    for trip in range(TRIPS):
        send_back(trip)

    def turn_copy(turn):
        return pltpu.make_async_remote_copy(
            src_ref=block.at[turn], dst_ref=turned.at[turn - 1],
            send_sem=turn_send.at[turn - 1], recv_sem=turn_recv.at[turn - 1],
            device_id=(place, rotated(me, turn, TA)), device_id_type=MESH,
        )

    @pl.loop(1, TA)
    def _(step):
        target = rotated(me, step, TA)
        gram_copy(COUNT - 1, me, target).wait_send()

    for chunk in range(CHUNKS - AHEAD, CHUNKS):
        all_lines(chunk).wait_send()
    for trip in range(TRIPS):
        out_all(trip).wait_send()
        back_all(trip).wait_send()

    for trip in range(TRIPS):
        columns = [column for part in GROUPED[trip] for column in range(*PARTS[part])]
        back_local(trip).wait()

        back_all(trip).wait_recv()

        @pl.loop(0, rows // 8)
        def _(step):
            for half in range(8 // piece):
                tile = owned[trip][step * (8 // piece) + half]
                for slot, column in enumerate(columns):
                    block[column, pl.ds(step * 8 + half * piece, piece), :] = tile[
                        :, slot * rows : (slot + 1) * rows
                    ]

        for column in columns:
            if 1 <= column <= turns:
                turn_copy(column).start()
        for column in columns:
            target = rotated(me, column, TA)
            out_ref[:, pl.ds(pl.multiple_of(target * rows, rows), rows)] = block[column]
        if trip == 0:
            for turn in range(1, turns + 1):
                turn_copy(turn).wait()
                target = rotated(me, TA - turn, TA)
                out_ref[:, pl.ds(pl.multiple_of(target * rows, rows), rows)] = turned[turn - 1].T


def on_device(field, weight, coef, window_start, window_end, owner_map):
    rows = field.shape[0]
    groups = lax.axis_size("gx")
    piece = rows // groups
    total = rows * TA
    lines = jnp.transpose(field, (1, 0, 2))
    vmem = pl.BlockSpec(memory_space=pltpu.VMEM)
    smem = pl.BlockSpec(memory_space=pltpu.SMEM)
    dma = pltpu.SemaphoreType.DMA
    turns = TA - KEPT
    widths = [(high - low) * rows for low, high in PARTS]
    trips = [sum(widths[part] for part in parts) for parts in GROUPED]

    def scratch(widths, *shape):
        return [pltpu.VMEM((*shape, width), jnp.float32) for width in widths]

    owned = pl.pallas_call(
        functools.partial(window_kernel, rows, total, groups),
        out_shape=jax.ShapeDtypeStruct((rows, total), jnp.float32),
        in_specs=[vmem, vmem, vmem, smem, smem, smem],
        out_specs=vmem,
        scratch_shapes=[
            pltpu.SMEM((groups,), jnp.int32),
            pltpu.VMEM((TA, rows, WIDTH), jnp.bfloat16),
            pltpu.VMEM((total, WIDTH), jnp.bfloat16),
            pltpu.VMEM((total, WIDTH), jnp.bfloat16),
            pltpu.VMEM((2 * BAND + 1, WIDTH), jnp.float32),
            pltpu.VMEM((1, WIDTH), jnp.float32),
            pltpu.VMEM((1, WIDTH), jnp.float32),
            pltpu.VMEM((total, PAIR * rows), jnp.float32),
            pltpu.VMEM((KEPT, rows, rows), jnp.float32),
            pltpu.VMEM((turns, rows, rows), jnp.float32),
            dma((CHUNKS,)), dma((CHUNKS,)), dma((CHUNKS,)),
            dma((COUNT, TA)), dma((COUNT, TA)), dma((COUNT,)),
            dma((COUNT, 2)), dma((COUNT, 2)),
            dma((TRIPS,)), dma((TRIPS,)), dma((TRIPS,)),
            dma((TRIPS,)), dma((TRIPS,)), dma((TRIPS,)),
            dma((turns,)), dma((turns,)),
            *scratch(widths, TA, rows),
            *scratch(widths, 3, rows),
            *scratch(widths, 2, rows),
            *scratch(trips, groups, piece),
            *scratch(trips, groups, piece),
            *scratch(trips, groups, piece),
            *scratch(trips, groups, piece),
        ],
        compiler_params=pltpu.CompilerParams(
            collective_id=0, has_side_effects=True, vmem_limit_bytes=48 * 1024 * 1024
        ),
        name="window_rows",
    )(lines, weight.reshape(WIDTH // 128, 128), coef, window_start, window_end, owner_map)
    return owned[None]


def solution(mesh):
    placed = (P("ta", None, "gx"), P("gx"), P(), P(), P(), P())
    return jax.shard_map(
        on_device, mesh=mesh, in_specs=placed, out_specs=P("gx", "ta", None), check_vma=False
    )
```

```python
import functools

import jax
import jax.numpy as jnp
from jax import lax
from jax.experimental import pallas as pl
from jax.experimental.pallas import tpu as pltpu
from jax.sharding import PartitionSpec as P

SPAN = 8
NYW = 224
BAND = 2
STATIONS = 8
WIDTH = STATIONS * NYW
TA = 8
MESH = pl.DeviceIdType.MESH
SENT = ((0, 1), (2, 3), (4, 5), (6,), (7,))
CUTS = (0, 384, 896, 1280, 1536, 1792)
DONE = (0, 256, 896, 1152, 1408, 1792)
CHUNKS = len(SENT)
AHEAD = 2
KEPT = 5
PAIR = 6
PARTS = ((1, 4), (4, 5), (0, 1))
COUNT = len(PARTS)
GROUPED = ((0,), (1, 2))
TRIPS = len(GROUPED)


def rotated(me, step, count):
    return lax.rem(me + step, count)


def window_kernel(
    rows, total, groups, x_ref, weight_ref, coef_ref, start_ref, end_ref, owner_ref, out_ref,
    source, send, lines, scaled, taps, mean, base, gram, block, turned,
    line_send, line_recv, line_own, gram_send, gram_recv, gram_own,
    side_send, side_recv, out_send, out_recv, out_own, back_send, back_recv, back_own,
    turn_send, turn_recv, *parts,
):
    place = lax.axis_index("gx")
    me = lax.axis_index("ta")
    tall = 2 * rows
    tile_rows = max(rows // 2, 16)
    piece = rows // groups
    turns = TA - KEPT
    landed, summed, beside = (parts[COUNT * kind : COUNT * (kind + 1)] for kind in range(3))
    parts = parts[COUNT * 3 :]
    pieces, spread, ordered, owned = (
        parts[TRIPS * kind : TRIPS * (kind + 1)] for kind in range(4)
    )

    barrier = pltpu.get_barrier_semaphore()

    @pl.loop(1, TA)
    def _(step):
        pl.semaphore_signal(
            barrier, inc=1, device_id=(place, rotated(me, step, TA)), device_id_type=MESH
        )

    @pl.loop(1, groups)
    def _(step):
        pl.semaphore_signal(
            barrier, inc=1, device_id=(rotated(place, step, groups), me), device_id_type=MESH
        )

    def line_copy(chunk, owner, target):
        lanes = slice(CUTS[chunk], CUTS[chunk + 1])
        return pltpu.make_async_remote_copy(
            src_ref=send.at[target, :, lanes],
            dst_ref=lines.at[pl.ds(pl.multiple_of(owner * rows, rows), rows), lanes],
            send_sem=line_send.at[chunk], recv_sem=line_recv.at[chunk],
            device_id=(place, target), device_id_type=MESH,
        )

    def all_lines(chunk):
        lanes = slice(CUTS[chunk], CUTS[chunk + 1])
        some = lines.at[: (TA - 1) * rows, lanes]
        return pltpu.make_async_remote_copy(
            src_ref=some, dst_ref=some,
            send_sem=line_send.at[chunk], recv_sem=line_recv.at[chunk],
            device_id=(place, me), device_id_type=MESH,
        )

    def own_copy(chunk):
        lanes = slice(CUTS[chunk], CUTS[chunk + 1])
        return pltpu.make_async_copy(
            send.at[me, :, lanes],
            lines.at[pl.ds(pl.multiple_of(me * rows, rows), rows), lanes],
            line_own.at[chunk],
        )

    def start_lines(chunk):
        @pl.loop(1, TA)
        def _(step):
            line_copy(chunk, me, rotated(me, step, TA)).start()

    for chunk in range(CHUNKS):
        for span in SENT[chunk]:

            @pl.loop(0, rows // tile_rows)
            def _(step):
                at = pl.ds(pl.multiple_of(step * tile_rows, tile_rows), tile_rows)
                tile = x_ref[span, at, :]
                for station in range(STATIONS):
                    send[station, at, NYW * span : NYW * (span + 1)] = tile[
                        :, NYW * station : NYW * (station + 1)
                    ]

        if chunk == 0:
            pl.semaphore_wait(barrier, TA - 1 + groups - 1)

        if chunk < AHEAD:
            start_lines(chunk)
        own_copy(chunk).start()

    for tile in range(WIDTH // 128):
        base[:1, 128 * tile : 128 * (tile + 1)] = weight_ref[tile : tile + 1, :]
    weight = jnp.zeros((1, NYW), jnp.float32)
    for station in range(STATIONS):
        weight = jnp.where(
            me == station, base[:1, NYW * station : NYW * (station + 1)], weight
        )
    reach = (
        lax.broadcasted_iota(jnp.int32, (2 * BAND + 1, NYW), 1)
        + lax.broadcasted_iota(jnp.int32, (2 * BAND + 1, NYW), 0) - BAND
    )
    tap = jnp.where((reach >= 0) & (reach < NYW), coef_ref[...], 0.0) * jnp.sqrt(weight)
    for span in range(SPAN):
        taps[:, NYW * span : NYW * (span + 1)] = tap

    def gram_rows(part, target):
        low, high = PARTS[part]
        begin = (lax.rem(target, 2) + low) * rows
        return gram.at[
            pl.ds(pl.multiple_of(target * rows, rows), rows),
            pl.ds(pl.multiple_of(begin, rows), (high - low) * rows),
        ]

    def gram_copy(part, owner, target):
        return pltpu.make_async_remote_copy(
            src_ref=gram_rows(part, target), dst_ref=landed[part].at[owner],
            send_sem=gram_send.at[part, target], recv_sem=gram_recv.at[part, owner],
            device_id=(place, target), device_id_type=MESH,
        )

    def gram_local(part):
        return pltpu.make_async_copy(gram_rows(part, me), landed[part].at[me], gram_own.at[part])

    def to_others(row, act):
        for side in range(2):
            target = 2 * row + side

            @pl.when(target != me)
            def _():
                act(target)

    pair = 2 * rows
    for chunk in range(CHUNKS):
        own_copy(chunk).wait()

        all_lines(chunk).wait_recv()

        if chunk + AHEAD < CHUNKS:
            all_lines(chunk).wait_send()
            start_lines(chunk + AHEAD)

        new = slice(CUTS[chunk], CUTS[chunk + 1])
        fresh = CUTS[chunk + 1] - CUTS[chunk]

        def add(step, acc):
            start = pl.multiple_of(step * 16, 16)
            tile = lines[pl.ds(start, 16), new].astype(jnp.float32)
            return acc + tile
        acc = lax.fori_loop(0, total // 16, add, jnp.zeros((16, fresh), jnp.float32), unroll=4)
        mean[:, new] = jnp.sum(acc, axis=0, keepdims=True) * (1.0 / total)

        first, last = DONE[chunk], DONE[chunk + 1]
        low = first if first % (4 * NYW) == 0 else first - 128
        high = last if last % (4 * NYW) == 0 else last + 128
        lanes = slice(first, last)

        middle = slice(first - low, last - low)
        level = mean[:, low:high]
        for offset in range(2 * BAND + 1):
            moved = level if offset == BAND else pltpu.roll(level, (BAND - offset) % (high - low), 1)
            base[offset : offset + 1, lanes] = moved[:, middle]

        @pl.loop(0, total // tall)
        def _(step):
            at = pl.ds(pl.multiple_of(step * tall, tall), tall)
            raw = lines[at, low:high]
            filtered = jnp.zeros((tall, last - first), jnp.float32)
            for offset in range(2 * BAND + 1):
                moved = raw if offset == BAND else pltpu.roll(raw, (BAND - offset) % (high - low), 1)
                centered = moved[:, middle].astype(jnp.float32) - base[offset : offset + 1, lanes]
                filtered = filtered + taps[offset : offset + 1, lanes] * centered
            scaled[at, lanes] = filtered.astype(jnp.bfloat16)

        def multiply(row, blocks):
            where = pl.ds(pl.multiple_of(row * pair, pair), pair)
            left = scaled[where, lanes]
            for index in blocks:
                column = lax.rem(row + index, TA // 2)
                right = scaled[pl.ds(pl.multiple_of(column * pair, pair), pair), lanes]
                product = lax.dot_general(
                    left, right, (((1,), (1,)), ((), ())), preferred_element_type=jnp.float32
                )
                at = slice(index * pair, (index + 1) * pair)
                if chunk == 0:
                    gram[where, at] = product
                else:
                    gram[where, at] = gram[where, at] + product

        if chunk < CHUNKS - 1:

            @pl.loop(0, TA // 2)
            def _(row):
                multiply(row, range(PAIR // 2))
        else:

            @pl.loop(1, TA // 2 + 1)
            def _(step):
                row = lax.rem(me // 2 + step, TA // 2)
                multiply(row, range(PAIR // 2))
                to_others(row, lambda target: gram_copy(0, me, target).start())

    for part in range(COUNT):
        gram_local(part).start()

    @pl.loop(0, groups)
    def _(slot):
        window = jnp.int32(0)
        for step in range(groups):
            window = jnp.where(owner_ref[step] == slot, step, window)
        source[slot] = window
    count = ((end_ref[place] - start_ref[place]) * (SPAN * NYW)).astype(jnp.float32)

    def follow(part):
        @pl.loop(1, TA // 2 + 1)
        def _(step):
            row = lax.rem(me // 2 + step, TA // 2)

            def act(target):
                gram_copy(part - 1, me, target).wait_send()
                gram_copy(part, me, target).start()
            to_others(row, act)

    next_start = jnp.where(
        place + 1 < groups, start_ref[jnp.minimum(place + 1, groups - 1)], groups * STATIONS
    )
    last_end = jnp.where(place > 0, end_ref[jnp.maximum(place - 1, 0)], 0)

    def shares(owner):
        station = place * STATIONS + owner
        upper = jnp.where(station >= next_start, 1.0, 0.0)
        lower = jnp.where(station < last_end, 1.0, 0.0)
        return upper, lower

    def reduce_part(part):
        land, total_of = landed[part], summed[part]
        gram_local(part).wait()
        upper, lower = shares(me)

        @pl.loop(0, rows // 8)
        def _(step):
            at = pl.ds(pl.multiple_of(step * 8, 8), 8)
            tile = land[me, at, :]
            total_of[0, at, :] = tile
            total_of[1, at, :] = tile * upper
            total_of[2, at, :] = tile * lower

        @pl.loop(1, TA)
        def _(count):
            owner = rotated(me, TA - count, TA)
            gram_copy(part, owner, me).wait_recv()
            upper, lower = shares(owner)

            @pl.loop(0, rows // 8)
            def _(step):
                at = pl.ds(pl.multiple_of(step * 8, 8), 8)
                tile = land[owner, at, :]
                total_of[0, at, :] = total_of[0, at, :] + tile
                total_of[1, at, :] = total_of[1, at, :] + tile * upper
                total_of[2, at, :] = total_of[2, at, :] + tile * lower

    after = rotated(place, 1, groups)
    before = rotated(place, groups - 1, groups)

    def side_copy(part, side):
        return pltpu.make_async_remote_copy(
            src_ref=summed[part].at[1 + side], dst_ref=beside[part].at[side],
            send_sem=side_send.at[part, side], recv_sem=side_recv.at[part, side],
            device_id=((after, before)[side], me), device_id_type=MESH,
        )

    def out_copy(part, owner, target):
        return pltpu.make_async_remote_copy(
            src_ref=pieces[part].at[target], dst_ref=spread[part].at[owner],
            send_sem=out_send.at[part], recv_sem=out_recv.at[part],
            device_id=(target, me), device_id_type=MESH,
        )

    def out_all(part):
        return pltpu.make_async_remote_copy(
            src_ref=pieces[part].at[: groups - 1], dst_ref=spread[part].at[: groups - 1],
            send_sem=out_send.at[part], recv_sem=out_recv.at[part],
            device_id=(place, me), device_id_type=MESH,
        )

    def back_all(part):
        return pltpu.make_async_remote_copy(
            src_ref=ordered[part].at[: groups - 1], dst_ref=owned[part].at[: groups - 1],
            send_sem=back_send.at[part], recv_sem=back_recv.at[part],
            device_id=(place, me), device_id_type=MESH,
        )

    def out_local(part):
        return pltpu.make_async_copy(
            pieces[part].at[place], spread[part].at[place], out_own.at[part]
        )

    def back_copy(part, owner, target):
        return pltpu.make_async_remote_copy(
            src_ref=ordered[part].at[target], dst_ref=owned[part].at[owner],
            send_sem=back_send.at[part], recv_sem=back_recv.at[part],
            device_id=(target, me), device_id_type=MESH,
        )

    def back_local(part):
        return pltpu.make_async_copy(
            ordered[part].at[place], owned[part].at[place], back_own.at[part]
        )

    def send_sides(part):
        reduce_part(part)
        for side in range(2):
            side_copy(part, side).start()

    def send_pieces(trip):
        for part in GROUPED[trip]:
            for side in range(2):
                side_copy(part, side).wait()
        scale = 1.0 / count

        @pl.loop(0, rows // 8)
        def _(step):
            at = pl.ds(pl.multiple_of(step * 8, 8), 8)
            begin = 0
            for part in GROUPED[trip]:
                tile = (
                    summed[part][0, at, :] + beside[part][0, at, :] + beside[part][1, at, :]
                ) * scale
                end = begin + tile.shape[1]
                for half in range(8 // piece):
                    pieces[trip][step * (8 // piece) + half, :, begin:end] = tile[
                        half * piece : (half + 1) * piece
                    ]
                begin = end

        @pl.loop(1, groups)
        def _(step):
            out_copy(trip, place, rotated(place, step, groups)).start()
        out_local(trip).start()

    def send_back(part):
        out_local(part).wait()

        out_all(part).wait_recv()

        @pl.loop(0, groups)
        def _(slot):
            ordered[part][slot] = spread[part][source[slot]]

        @pl.loop(1, groups)
        def _(step):
            back_copy(part, place, rotated(place, step, groups)).start()
        back_local(part).start()

    follow(1)
    send_sides(0)
    follow(2)
    send_sides(1)
    send_pieces(0)
    send_sides(2)
    send_pieces(1)
    for trip in range(TRIPS):
        send_back(trip)

    def turn_copy(turn):
        return pltpu.make_async_remote_copy(
            src_ref=block.at[turn], dst_ref=turned.at[turn - 1],
            send_sem=turn_send.at[turn - 1], recv_sem=turn_recv.at[turn - 1],
            device_id=(place, rotated(me, turn, TA)), device_id_type=MESH,
        )

    @pl.loop(1, TA)
    def _(step):
        target = rotated(me, step, TA)
        gram_copy(COUNT - 1, me, target).wait_send()

    for chunk in range(CHUNKS - AHEAD, CHUNKS):
        all_lines(chunk).wait_send()
    for trip in range(TRIPS):
        out_all(trip).wait_send()
        back_all(trip).wait_send()

    for trip in range(TRIPS):
        columns = [column for part in GROUPED[trip] for column in range(*PARTS[part])]
        back_local(trip).wait()

        back_all(trip).wait_recv()

        @pl.loop(0, rows // 8)
        def _(step):
            for half in range(8 // piece):
                tile = owned[trip][step * (8 // piece) + half]
                for slot, column in enumerate(columns):
                    block[column, pl.ds(step * 8 + half * piece, piece), :] = tile[
                        :, slot * rows : (slot + 1) * rows
                    ]

        for column in columns:
            if 1 <= column <= turns:
                turn_copy(column).start()
        for column in columns:
            target = rotated(me, column, TA)
            out_ref[:, pl.ds(pl.multiple_of(target * rows, rows), rows)] = block[column]
        if trip == 0:
            for turn in range(1, turns + 1):
                turn_copy(turn).wait()
                target = rotated(me, TA - turn, TA)
                out_ref[:, pl.ds(pl.multiple_of(target * rows, rows), rows)] = turned[turn - 1].T


def on_device(field, weight, coef, window_start, window_end, owner_map):
    rows = field.shape[0]
    groups = lax.axis_size("gx")
    piece = rows // groups
    total = rows * TA
    lines = jnp.transpose(field, (1, 0, 2))
    vmem = pl.BlockSpec(memory_space=pltpu.VMEM)
    smem = pl.BlockSpec(memory_space=pltpu.SMEM)
    dma = pltpu.SemaphoreType.DMA
    turns = TA - KEPT
    widths = [(high - low) * rows for low, high in PARTS]
    trips = [sum(widths[part] for part in parts) for parts in GROUPED]

    def scratch(widths, *shape):
        return [pltpu.VMEM((*shape, width), jnp.float32) for width in widths]

    owned = pl.pallas_call(
        functools.partial(window_kernel, rows, total, groups),
        out_shape=jax.ShapeDtypeStruct((rows, total), jnp.float32),
        in_specs=[vmem, vmem, vmem, smem, smem, smem],
        out_specs=vmem,
        scratch_shapes=[
            pltpu.SMEM((groups,), jnp.int32),
            pltpu.VMEM((TA, rows, WIDTH), jnp.bfloat16),
            pltpu.VMEM((total, WIDTH), jnp.bfloat16),
            pltpu.VMEM((total, WIDTH), jnp.bfloat16),
            pltpu.VMEM((2 * BAND + 1, WIDTH), jnp.float32),
            pltpu.VMEM((1, WIDTH), jnp.float32),
            pltpu.VMEM((2 * BAND + 1, WIDTH), jnp.float32),
            pltpu.VMEM((total, PAIR * rows), jnp.float32),
            pltpu.VMEM((KEPT, rows, rows), jnp.float32),
            pltpu.VMEM((turns, rows, rows), jnp.float32),
            dma((CHUNKS,)), dma((CHUNKS,)), dma((CHUNKS,)),
            dma((COUNT, TA)), dma((COUNT, TA)), dma((COUNT,)),
            dma((COUNT, 2)), dma((COUNT, 2)),
            dma((TRIPS,)), dma((TRIPS,)), dma((TRIPS,)),
            dma((TRIPS,)), dma((TRIPS,)), dma((TRIPS,)),
            dma((turns,)), dma((turns,)),
            *scratch(widths, TA, rows),
            *scratch(widths, 3, rows),
            *scratch(widths, 2, rows),
            *scratch(trips, groups, piece),
            *scratch(trips, groups, piece),
            *scratch(trips, groups, piece),
            *scratch(trips, groups, piece),
        ],
        compiler_params=pltpu.CompilerParams(
            collective_id=0, has_side_effects=True, vmem_limit_bytes=48 * 1024 * 1024
        ),
        name="window_rows",
    )(lines, weight.reshape(WIDTH // 128, 128), coef, window_start, window_end, owner_map)
    return owned[None]


def solution(mesh):
    placed = (P("ta", None, "gx"), P("gx"), P(), P(), P(), P())
    return jax.shard_map(
        on_device, mesh=mesh, in_specs=placed, out_specs=P("gx", "ta", None), check_vma=False
    )
```

```python
import functools

import jax
import jax.numpy as jnp
from jax import lax
from jax.experimental import pallas as pl
from jax.experimental.pallas import tpu as pltpu
from jax.sharding import PartitionSpec as P

SPAN = 8
NYW = 224
BAND = 2
STATIONS = 8
WIDTH = STATIONS * NYW
TA = 8
MESH = pl.DeviceIdType.MESH
SENT = ((0, 1), (2, 3), (4, 5), (6,), (7,))
CUTS = (0, 384, 896, 1280, 1536, 1792)
DONE = (0, 256, 896, 1152, 1408, 1792)
CHUNKS = len(SENT)
AHEAD = 2
KEPT = 5
PAIR = 6
PARTS = ((1, 4), (4, 5), (0, 1))
COUNT = len(PARTS)
GROUPED = ((0,), (1, 2))
TRIPS = len(GROUPED)


def rotated(me, step, count):
    return lax.rem(me + step, count)


def window_kernel(
    rows, total, groups, x_ref, weight_ref, coef_ref, start_ref, end_ref, owner_ref, out_ref,
    source, send, lines, scaled, taps, mean, base, gram, block, turned,
    line_send, line_recv, line_own, gram_send, gram_recv, gram_own,
    side_send, side_recv, out_send, out_recv, out_own, back_send, back_recv, back_own,
    turn_send, turn_recv, *parts,
):
    place = lax.axis_index("gx")
    me = lax.axis_index("ta")
    tall = 2 * rows
    tile_rows = max(rows // 2, 16)
    piece = rows // groups
    turns = TA - KEPT
    landed, summed, beside = (parts[COUNT * kind : COUNT * (kind + 1)] for kind in range(3))
    parts = parts[COUNT * 3 :]
    pieces, spread, ordered, owned = (
        parts[TRIPS * kind : TRIPS * (kind + 1)] for kind in range(4)
    )

    barrier = pltpu.get_barrier_semaphore()

    @pl.loop(1, TA)
    def _(step):
        pl.semaphore_signal(
            barrier, inc=1, device_id=(place, rotated(me, step, TA)), device_id_type=MESH
        )

    @pl.loop(1, groups, unroll=True)
    def _(step):
        pl.semaphore_signal(
            barrier, inc=1, device_id=(rotated(place, step, groups), me), device_id_type=MESH
        )

    def line_copy(chunk, owner, target):
        lanes = slice(CUTS[chunk], CUTS[chunk + 1])
        return pltpu.make_async_remote_copy(
            src_ref=send.at[target, :, lanes],
            dst_ref=lines.at[pl.ds(pl.multiple_of(owner * rows, rows), rows), lanes],
            send_sem=line_send.at[chunk], recv_sem=line_recv.at[chunk],
            device_id=(place, target), device_id_type=MESH,
        )

    def all_lines(chunk):
        lanes = slice(CUTS[chunk], CUTS[chunk + 1])
        some = lines.at[: (TA - 1) * rows, lanes]
        return pltpu.make_async_remote_copy(
            src_ref=some, dst_ref=some,
            send_sem=line_send.at[chunk], recv_sem=line_recv.at[chunk],
            device_id=(place, me), device_id_type=MESH,
        )

    def own_copy(chunk):
        lanes = slice(CUTS[chunk], CUTS[chunk + 1])
        return pltpu.make_async_copy(
            send.at[me, :, lanes],
            lines.at[pl.ds(pl.multiple_of(me * rows, rows), rows), lanes],
            line_own.at[chunk],
        )

    def start_lines(chunk):
        @pl.loop(1, TA)
        def _(step):
            line_copy(chunk, me, rotated(me, step, TA)).start()

    for chunk in range(CHUNKS):
        for span in SENT[chunk]:

            @pl.loop(0, rows // tile_rows)
            def _(step):
                at = pl.ds(pl.multiple_of(step * tile_rows, tile_rows), tile_rows)
                tile = x_ref[span, at, :]
                for station in range(STATIONS):
                    send[station, at, NYW * span : NYW * (span + 1)] = tile[
                        :, NYW * station : NYW * (station + 1)
                    ]

        if chunk == 0:
            pl.semaphore_wait(barrier, TA - 1 + groups - 1)

        if chunk < AHEAD:
            start_lines(chunk)
        own_copy(chunk).start()

    for tile in range(WIDTH // 128):
        base[:1, 128 * tile : 128 * (tile + 1)] = weight_ref[tile : tile + 1, :]
    weight = jnp.zeros((1, NYW), jnp.float32)
    for station in range(STATIONS):
        weight = jnp.where(
            me == station, base[:1, NYW * station : NYW * (station + 1)], weight
        )
    reach = (
        lax.broadcasted_iota(jnp.int32, (2 * BAND + 1, NYW), 1)
        + lax.broadcasted_iota(jnp.int32, (2 * BAND + 1, NYW), 0) - BAND
    )
    tap = jnp.where((reach >= 0) & (reach < NYW), coef_ref[...], 0.0) * jnp.sqrt(weight)
    for span in range(SPAN):
        taps[:, NYW * span : NYW * (span + 1)] = tap

    def gram_rows(part, target):
        low, high = PARTS[part]
        begin = (lax.rem(target, 2) + low) * rows
        return gram.at[
            pl.ds(pl.multiple_of(target * rows, rows), rows),
            pl.ds(pl.multiple_of(begin, rows), (high - low) * rows),
        ]

    def gram_copy(part, owner, target):
        return pltpu.make_async_remote_copy(
            src_ref=gram_rows(part, target), dst_ref=landed[part].at[owner],
            send_sem=gram_send.at[part, target], recv_sem=gram_recv.at[part, owner],
            device_id=(place, target), device_id_type=MESH,
        )

    def gram_local(part):
        return pltpu.make_async_copy(gram_rows(part, me), landed[part].at[me], gram_own.at[part])

    def to_others(row, act):
        for side in range(2):
            target = 2 * row + side

            @pl.when(target != me)
            def _():
                act(target)

    pair = 2 * rows
    for chunk in range(CHUNKS):
        own_copy(chunk).wait()

        all_lines(chunk).wait_recv()

        if chunk + AHEAD < CHUNKS:
            all_lines(chunk).wait_send()
            start_lines(chunk + AHEAD)

        new = slice(CUTS[chunk], CUTS[chunk + 1])
        fresh = CUTS[chunk + 1] - CUTS[chunk]

        def add(step, acc):
            start = pl.multiple_of(step * 16, 16)
            tile = lines[pl.ds(start, 16), new].astype(jnp.float32)
            return acc + tile
        acc = lax.fori_loop(0, total // 16, add, jnp.zeros((16, fresh), jnp.float32), unroll=4)
        mean[:, new] = jnp.sum(acc, axis=0, keepdims=True) * (1.0 / total)

        first, last = DONE[chunk], DONE[chunk + 1]
        low = first if first % (4 * NYW) == 0 else first - 128
        high = last if last % (4 * NYW) == 0 else last + 128
        lanes = slice(first, last)

        middle = slice(first - low, last - low)
        level = mean[:, low:high]
        for offset in range(2 * BAND + 1):
            moved = level if offset == BAND else pltpu.roll(level, (BAND - offset) % (high - low), 1)
            base[offset : offset + 1, lanes] = moved[:, middle]

        @pl.loop(0, total // tall)
        def _(step):
            at = pl.ds(pl.multiple_of(step * tall, tall), tall)
            raw = lines[at, low:high]
            filtered = jnp.zeros((tall, last - first), jnp.float32)
            for offset in range(2 * BAND + 1):
                moved = raw if offset == BAND else pltpu.roll(raw, (BAND - offset) % (high - low), 1)
                centered = moved[:, middle].astype(jnp.float32) - base[offset : offset + 1, lanes]
                filtered = filtered + taps[offset : offset + 1, lanes] * centered
            scaled[at, lanes] = filtered.astype(jnp.bfloat16)

        def multiply(row, blocks):
            where = pl.ds(pl.multiple_of(row * pair, pair), pair)
            left = scaled[where, lanes]
            for index in blocks:
                column = lax.rem(row + index, TA // 2)
                right = scaled[pl.ds(pl.multiple_of(column * pair, pair), pair), lanes]
                product = lax.dot_general(
                    left, right, (((1,), (1,)), ((), ())), preferred_element_type=jnp.float32
                )
                at = slice(index * pair, (index + 1) * pair)
                if chunk == 0:
                    gram[where, at] = product
                else:
                    gram[where, at] = gram[where, at] + product

        if chunk < CHUNKS - 1:

            @pl.loop(0, TA // 2)
            def _(row):
                multiply(row, range(PAIR // 2))
        else:

            @pl.loop(1, TA // 2 + 1)
            def _(step):
                row = lax.rem(me // 2 + step, TA // 2)
                multiply(row, range(PAIR // 2))
                to_others(row, lambda target: gram_copy(0, me, target).start())

    for part in range(COUNT):
        gram_local(part).start()

    @pl.loop(0, groups)
    def _(slot):
        window = jnp.int32(0)
        for step in range(groups):
            window = jnp.where(owner_ref[step] == slot, step, window)
        source[slot] = window
    count = ((end_ref[place] - start_ref[place]) * (SPAN * NYW)).astype(jnp.float32)

    def follow(part):
        @pl.loop(1, TA // 2 + 1)
        def _(step):
            row = lax.rem(me // 2 + step, TA // 2)

            def act(target):
                gram_copy(part - 1, me, target).wait_send()
                gram_copy(part, me, target).start()
            to_others(row, act)

    next_start = jnp.where(
        place + 1 < groups, start_ref[jnp.minimum(place + 1, groups - 1)], groups * STATIONS
    )
    last_end = jnp.where(place > 0, end_ref[jnp.maximum(place - 1, 0)], 0)

    def shares(owner):
        station = place * STATIONS + owner
        upper = jnp.where(station >= next_start, 1.0, 0.0)
        lower = jnp.where(station < last_end, 1.0, 0.0)
        return upper, lower

    def reduce_part(part):
        land, total_of = landed[part], summed[part]
        gram_local(part).wait()
        upper, lower = shares(me)

        @pl.loop(0, rows // 8)
        def _(step):
            at = pl.ds(pl.multiple_of(step * 8, 8), 8)
            tile = land[me, at, :]
            total_of[0, at, :] = tile
            total_of[1, at, :] = tile * upper
            total_of[2, at, :] = tile * lower

        @pl.loop(1, TA)
        def _(count):
            owner = rotated(me, TA - count, TA)
            gram_copy(part, owner, me).wait_recv()
            upper, lower = shares(owner)

            @pl.loop(0, rows // 8)
            def _(step):
                at = pl.ds(pl.multiple_of(step * 8, 8), 8)
                tile = land[owner, at, :]
                total_of[0, at, :] = total_of[0, at, :] + tile
                total_of[1, at, :] = total_of[1, at, :] + tile * upper
                total_of[2, at, :] = total_of[2, at, :] + tile * lower

    after = rotated(place, 1, groups)
    before = rotated(place, groups - 1, groups)

    def side_copy(part, side):
        return pltpu.make_async_remote_copy(
            src_ref=summed[part].at[1 + side], dst_ref=beside[part].at[side],
            send_sem=side_send.at[part, side], recv_sem=side_recv.at[part, side],
            device_id=((after, before)[side], me), device_id_type=MESH,
        )

    def out_copy(part, owner, target):
        return pltpu.make_async_remote_copy(
            src_ref=pieces[part].at[target], dst_ref=spread[part].at[owner],
            send_sem=out_send.at[part], recv_sem=out_recv.at[part],
            device_id=(target, me), device_id_type=MESH,
        )

    def out_all(part):
        return pltpu.make_async_remote_copy(
            src_ref=pieces[part].at[: groups - 1], dst_ref=spread[part].at[: groups - 1],
            send_sem=out_send.at[part], recv_sem=out_recv.at[part],
            device_id=(place, me), device_id_type=MESH,
        )

    def back_all(part):
        return pltpu.make_async_remote_copy(
            src_ref=ordered[part].at[: groups - 1], dst_ref=owned[part].at[: groups - 1],
            send_sem=back_send.at[part], recv_sem=back_recv.at[part],
            device_id=(place, me), device_id_type=MESH,
        )

    def out_local(part):
        return pltpu.make_async_copy(
            pieces[part].at[place], spread[part].at[place], out_own.at[part]
        )

    def back_copy(part, owner, target):
        return pltpu.make_async_remote_copy(
            src_ref=ordered[part].at[target], dst_ref=owned[part].at[owner],
            send_sem=back_send.at[part], recv_sem=back_recv.at[part],
            device_id=(target, me), device_id_type=MESH,
        )

    def back_local(part):
        return pltpu.make_async_copy(
            ordered[part].at[place], owned[part].at[place], back_own.at[part]
        )

    def send_sides(part):
        reduce_part(part)
        for side in range(2):
            side_copy(part, side).start()

    def send_pieces(trip):
        for part in GROUPED[trip]:
            for side in range(2):
                side_copy(part, side).wait()
        scale = 1.0 / count

        @pl.loop(0, rows // 8)
        def _(step):
            at = pl.ds(pl.multiple_of(step * 8, 8), 8)
            begin = 0
            for part in GROUPED[trip]:
                tile = (
                    summed[part][0, at, :] + beside[part][0, at, :] + beside[part][1, at, :]
                ) * scale
                end = begin + tile.shape[1]
                for half in range(8 // piece):
                    pieces[trip][step * (8 // piece) + half, :, begin:end] = tile[
                        half * piece : (half + 1) * piece
                    ]
                begin = end

        @pl.loop(1, groups, unroll=True)
        def _(step):
            out_copy(trip, place, rotated(place, step, groups)).start()
        out_local(trip).start()

    def send_back(part):
        out_local(part).wait()

        out_all(part).wait_recv()

        @pl.loop(0, groups)
        def _(slot):
            ordered[part][slot] = spread[part][source[slot]]

        @pl.loop(1, groups, unroll=True)
        def _(step):
            back_copy(part, place, rotated(place, step, groups)).start()
        back_local(part).start()

    follow(1)
    send_sides(0)
    follow(2)
    send_sides(1)
    send_pieces(0)
    send_sides(2)
    send_pieces(1)
    for trip in range(TRIPS):
        send_back(trip)

    def turn_copy(turn):
        return pltpu.make_async_remote_copy(
            src_ref=block.at[turn], dst_ref=turned.at[turn - 1],
            send_sem=turn_send.at[turn - 1], recv_sem=turn_recv.at[turn - 1],
            device_id=(place, rotated(me, turn, TA)), device_id_type=MESH,
        )

    @pl.loop(1, TA)
    def _(step):
        target = rotated(me, step, TA)
        gram_copy(COUNT - 1, me, target).wait_send()

    for chunk in range(CHUNKS - AHEAD, CHUNKS):
        all_lines(chunk).wait_send()
    for trip in range(TRIPS):
        out_all(trip).wait_send()
        back_all(trip).wait_send()

    for trip in range(TRIPS):
        columns = [column for part in GROUPED[trip] for column in range(*PARTS[part])]
        back_local(trip).wait()

        back_all(trip).wait_recv()

        @pl.loop(0, rows // 8)
        def _(step):
            for half in range(8 // piece):
                tile = owned[trip][step * (8 // piece) + half]
                for slot, column in enumerate(columns):
                    block[column, pl.ds(step * 8 + half * piece, piece), :] = tile[
                        :, slot * rows : (slot + 1) * rows
                    ]

        for column in columns:
            if 1 <= column <= turns:
                turn_copy(column).start()
        for column in columns:
            target = rotated(me, column, TA)
            out_ref[:, pl.ds(pl.multiple_of(target * rows, rows), rows)] = block[column]
        if trip == 0:
            for turn in range(1, turns + 1):
                turn_copy(turn).wait()
                target = rotated(me, TA - turn, TA)
                out_ref[:, pl.ds(pl.multiple_of(target * rows, rows), rows)] = turned[turn - 1].T


def on_device(field, weight, coef, window_start, window_end, owner_map):
    rows = field.shape[0]
    groups = lax.axis_size("gx")
    piece = rows // groups
    total = rows * TA
    lines = jnp.transpose(field, (1, 0, 2))
    vmem = pl.BlockSpec(memory_space=pltpu.VMEM)
    smem = pl.BlockSpec(memory_space=pltpu.SMEM)
    dma = pltpu.SemaphoreType.DMA
    turns = TA - KEPT
    widths = [(high - low) * rows for low, high in PARTS]
    trips = [sum(widths[part] for part in parts) for parts in GROUPED]

    def scratch(widths, *shape):
        return [pltpu.VMEM((*shape, width), jnp.float32) for width in widths]

    owned = pl.pallas_call(
        functools.partial(window_kernel, rows, total, groups),
        out_shape=jax.ShapeDtypeStruct((rows, total), jnp.float32),
        in_specs=[vmem, vmem, vmem, smem, smem, smem],
        out_specs=vmem,
        scratch_shapes=[
            pltpu.SMEM((groups,), jnp.int32),
            pltpu.VMEM((TA, rows, WIDTH), jnp.bfloat16),
            pltpu.VMEM((total, WIDTH), jnp.bfloat16),
            pltpu.VMEM((total, WIDTH), jnp.bfloat16),
            pltpu.VMEM((2 * BAND + 1, WIDTH), jnp.float32),
            pltpu.VMEM((1, WIDTH), jnp.float32),
            pltpu.VMEM((2 * BAND + 1, WIDTH), jnp.float32),
            pltpu.VMEM((total, PAIR * rows), jnp.float32),
            pltpu.VMEM((KEPT, rows, rows), jnp.float32),
            pltpu.VMEM((turns, rows, rows), jnp.float32),
            dma((CHUNKS,)), dma((CHUNKS,)), dma((CHUNKS,)),
            dma((COUNT, TA)), dma((COUNT, TA)), dma((COUNT,)),
            dma((COUNT, 2)), dma((COUNT, 2)),
            dma((TRIPS,)), dma((TRIPS,)), dma((TRIPS,)),
            dma((TRIPS,)), dma((TRIPS,)), dma((TRIPS,)),
            dma((turns,)), dma((turns,)),
            *scratch(widths, TA, rows),
            *scratch(widths, 3, rows),
            *scratch(widths, 2, rows),
            *scratch(trips, groups, piece),
            *scratch(trips, groups, piece),
            *scratch(trips, groups, piece),
            *scratch(trips, groups, piece),
        ],
        compiler_params=pltpu.CompilerParams(
            collective_id=0, has_side_effects=True, vmem_limit_bytes=48 * 1024 * 1024
        ),
        name="window_rows",
    )(lines, weight.reshape(WIDTH // 128, 128), coef, window_start, window_end, owner_map)
    return owned[None]


def solution(mesh):
    placed = (P("ta", None, "gx"), P("gx"), P(), P(), P(), P())
    return jax.shard_map(
        on_device, mesh=mesh, in_specs=placed, out_specs=P("gx", "ta", None), check_vma=False
    )
```
